256 devices in a mesh: rep: 32 (over z, y), rack: 8 (over x, core).
Axes of the slice: x: 4, y: 4, z: 8, core: 2. Of those that a mesh axis runs over, the one named last changes fastest.
Arguments:
- grads: bfloat16 [64, 1024, 1024], P('rep', 'rack'), may hold values from -3 to 3
- left: bfloat16 [64, 1024, 1024], P('rep', 'rack'), may hold values from -1 to 3, as said below
- right: bfloat16 [64, 1024, 1024], P('rep', 'rack'), may hold values from -1 to 3, as said below
- left_root: bfloat16 [64, 1024, 1024], P('rep', 'rack'), may hold values from -1 to 3, as said below
- right_root: bfloat16 [64, 1024, 1024], P('rep', 'rack'), may hold values from -1 to 3, as said below
- second: bfloat16 [64, 1024, 1024], P('rep', 'rack'), may hold values from 9.9658966e-05 to 0.0099487305
- owner: int32 [32], replicated, may hold values from 0 to 31, as said below
Outputs:
- left_new: bfloat16 [64, 1024, 1024], P('rep', 'rack')
- right_new: bfloat16 [64, 1024, 1024], P('rep', 'rack')
- second_new: bfloat16 [64, 1024, 1024], P('rep', 'rack')
- directions: bfloat16 [32, 1024, 1024], P(None, 'rack')
The draws below stay inside these ranges and needn't reach their ends.
Inputs may be any that keep to these rules, and one draw needn't show every extreme that they name: Each owner holds at most 2 blocks and some owner holds exactly 2. `left`: symmetric in the last two dimensions. `right`: symmetric in the last two dimensions. `left_root`: symmetric in the last two dimensions. `right_root`: symmetric in the last two dimensions.
All inputs are finite; a program needn't handle non-finite values.
Results may differ from the reference program's by a relative error of at most 0.017.
Values may be sent and summed in bfloat16 or wider, within the bound.
A program may use at most 128 MiB of HBM per device.

```python
import math
import jax
import jax.numpy as jnp
from jax import lax

BLOCK = 1024
BLOCKS = 32
SLOTS_DEV = 2
SLOTS = 64
N_REP = 32


def symmetric_draw(key, low, high, spread):
    key_diag, key_off = jax.random.split(key)
    shape = (SLOTS, BLOCK, BLOCK)
    diag = jnp.exp(jax.random.uniform(key_diag, (SLOTS, BLOCK), jnp.float32, math.log(low), math.log(high)))
    raw = jnp.clip(jax.random.normal(key_off, shape, jnp.float32), -5.0, 5.0)
    sym = (raw + jnp.swapaxes(raw, 1, 2)) * (spread / math.sqrt(2.0 * BLOCK))
    rows = lax.broadcasted_iota(jnp.int32, (BLOCK, BLOCK), 0)
    cols = lax.broadcasted_iota(jnp.int32, (BLOCK, BLOCK), 1)
    eye = (rows == cols).astype(jnp.float32)
    return sym + diag[:, :, None] * eye[None]


def draw_grads(key, part):
    key = jax.random.fold_in(key, 11)
    key_z, key_r, key_c = jax.random.split(key, 3)
    shape = (SLOTS, BLOCK, BLOCK)
    base = jnp.clip(jax.random.normal(key_z, shape, jnp.float32), -5.0, 5.0)
    row_scale = jnp.exp(jax.random.uniform(key_r, (SLOTS, BLOCK, 1), jnp.float32, 0.0, math.log(10.0)))
    position = lax.broadcasted_iota(jnp.float32, (1, BLOCK, 1), 1)
    row_scale = row_scale * jnp.sqrt(1.0 + 2.0 * position / BLOCK)
    col_scale = jnp.exp(jax.random.uniform(key_c, (SLOTS, 1, BLOCK), jnp.float32, 0.0, math.log(10.0)))
    grad = base * row_scale * col_scale / (10.0 * math.sqrt(BLOCK))
    return jnp.clip(grad, -3.0, 3.0).astype(jnp.bfloat16)


def draw_left(key, part):
    key = jax.random.fold_in(key, 21)
    return symmetric_draw(key, 0.5, 2.0, 0.4).astype(jnp.bfloat16)


def draw_right(key, part):
    key = jax.random.fold_in(key, 31)
    return symmetric_draw(key, 0.5, 2.0, 0.4).astype(jnp.bfloat16)


def draw_left_root(key, part):
    key = jax.random.fold_in(key, 41)
    return symmetric_draw(key, 1.0, 2.0, 0.4).astype(jnp.bfloat16)


def draw_right_root(key, part):
    key = jax.random.fold_in(key, 51)
    return symmetric_draw(key, 1.0, 2.0, 0.4).astype(jnp.bfloat16)


def draw_owner(key, part):
    key = jax.random.fold_in(key, 61)
    key_perm, key_full, key_order = jax.random.split(key, 3)
    owners_perm = jax.random.permutation(key_perm, N_REP).astype(jnp.int32)
    full_count = jax.random.randint(key_full, (), 1, N_REP // 2 + 1).astype(jnp.int32)
    spots = jnp.arange(BLOCKS, dtype=jnp.int32)
    in_full = spots < full_count * SLOTS_DEV
    rest = (spots - full_count * SLOTS_DEV) % (N_REP - full_count)
    which = jnp.where(in_full, spots // SLOTS_DEV, full_count + rest).astype(jnp.int32)
    base = owners_perm[which]
    order = jax.random.permutation(key_order, BLOCKS).astype(jnp.int32)
    return base[order].astype(jnp.int32)


def block_scale(rng, dims, cuts, smallest, high):
    def one(axis_at, blocks):
        heights = jax.random.uniform(jax.random.fold_in(jax.random.fold_in(rng, 6), axis_at), (blocks,), jnp.float32, smallest / len(cuts), high / len(cuts))
        return jnp.repeat(jnp.exp(heights), dims[axis_at] // blocks).reshape((-1,) + (1,) * (len(dims) - axis_at - 1))

    loudness = one(*cuts[0])
    for cut in cuts[1:]:
        loudness = loudness * one(*cut)
    return loudness


def setup_inputs(seed: int = 0) -> dict:
    keys = jax.random.split(jax.random.key(seed), 8)
    grads = draw_grads(jax.random.fold_in(keys[7], 71), 0)
    left = draw_left(jax.random.fold_in(keys[7], 71), 0)
    right = draw_right(jax.random.fold_in(keys[7], 71), 0)
    left_root = draw_left_root(jax.random.fold_in(keys[7], 71), 0)
    right_root = draw_right_root(jax.random.fold_in(keys[7], 71), 0)
    second = jnp.clip(jnp.exp(math.log(0.0099487305) - 4.603446 * jax.random.uniform(keys[5], (SLOTS, BLOCK, BLOCK), jnp.float32) ** block_scale(keys[5], (SLOTS, BLOCK, BLOCK), ((0, 32), (1, 8)), -0.2, 0.2)), 9.965896606445312e-05, 0.0099487305).astype(jnp.bfloat16)
    owner = draw_owner(jax.random.fold_in(keys[7], 71), 0)
    return dict(grads=grads, left=left, right=right, left_root=left_root, right_root=right_root, second=second, owner=owner)


def one_block(grad, left_f, right_f, left_r, right_r, moment_old):
    outer = jnp.dot(grad, grad.T, preferred_element_type=jnp.float32)
    inner = jnp.dot(grad.T, grad, preferred_element_type=jnp.float32)
    left_out = (0.95 * left_f.astype(jnp.float32) + 0.05 * outer).astype(jnp.bfloat16)
    right_out = (0.95 * right_f.astype(jnp.float32) + 0.05 * inner).astype(jnp.bfloat16)
    mixed = jnp.dot(left_r, grad, preferred_element_type=jnp.float32).astype(jnp.bfloat16)
    prec = jnp.dot(mixed, right_r, preferred_element_type=jnp.float32)
    prec_b = lax.optimization_barrier(prec.astype(jnp.bfloat16))
    grad32 = grad.astype(jnp.float32)
    moment = 0.95 * moment_old.astype(jnp.float32) + 0.05 * grad32 * grad32
    adam = grad32 / (jnp.sqrt(moment) + 1e-08)
    scale = jnp.sqrt(jnp.sum(adam * adam)) / jnp.sqrt(jnp.sum(prec * prec) + 1e-06)
    direction = (prec_b.astype(jnp.float32) * scale).astype(jnp.bfloat16)
    return (left_out, right_out, moment.astype(jnp.bfloat16), direction)

def reference(grads, left, right, left_root, right_root, second, owner):
    count = owner.shape[0]
    spots = jnp.arange(count, dtype=jnp.int32)
    earlier = (owner[None, :] == owner[:, None]) & (spots[None, :] < spots[:, None])
    slot = lax.optimization_barrier(jnp.sum(earlier.astype(jnp.int32), axis=1)).astype(jnp.int32)
    place = (owner * SLOTS_DEV + slot).astype(jnp.int32)

    def step_one(index):
        return one_block(grads[index], left[index], right[index], left_root[index], right_root[index], second[index])
    left_out, right_out, moment_out, directions = lax.map(step_one, place)
    left_new = left.at[place].set(left_out)
    right_new = right.at[place].set(right_out)
    second_new = second.at[place].set(moment_out)
    return (left_new, right_new, second_new, directions)
```

```python
import functools

import jax
import jax.numpy as jnp
from jax import lax
from jax.experimental import pallas as pl
from jax.experimental.pallas import tpu as pltpu
from jax.sharding import PartitionSpec as P

MESH = pl.DeviceIdType.MESH
BF, F32, I32 = jnp.bfloat16, jnp.float32, jnp.int32

NX, NY, NZ = 4, 4, 8
ROWS, WIDTH, SLOTS_DEV = 128, 1024, 2
HALF_A = 192
QUARTER = 160
HALF_B = QUARTER // 2
FIRST_B = 2 * HALF_A
CHUNK = HALF_A + HALF_B
OWN = SLOTS_DEV * NY
LAG = 3
LAG_Y = 3
SECOND = 12
STEPS = 46
KEEP = 8
ORDER = (
    (0, 0), (0, 1), (0, 2), (0, 3), (1, 0), (0, 4), (1, 1), (0, 5), (1, 2), (0, 6), (1, 3), (1, 4), (1, 5), (1, 6),
)


def me():
    rep, rack = lax.axis_index("rep"), lax.axis_index("rack")
    return rep // NY, rep % NY, rack // 2, rack % 2


def dev(z, y, x, c):
    return (z * NY + y, x * 2 + c)


def rcopy(src, dst, send, recv, to):
    return pltpu.make_async_remote_copy(
        src_ref=src, dst_ref=dst, send_sem=send, recv_sem=recv, device_id=to, device_id_type=MESH
    )


def schedule(owner_row, owner_col, z, y):
    row = lax.broadcasted_iota(I32, (8, 128), 0)
    lane = lax.broadcasted_iota(I32, (8, 128), 1)
    own = jnp.broadcast_to(owner_row, (8, 128))
    cnt = [
        jnp.broadcast_to(
            jnp.sum((own == row * NY + k).astype(I32), axis=1, keepdims=True), (8, 128)
        )
        for k in range(NY)
    ]
    used = [[(c > p).astype(I32) for c in cnt] for p in range(SLOTS_DEV)]
    size = [u[0] + u[1] + u[2] + u[3] for u in used]
    before = [[sum(u[:k], jnp.zeros((8, 128), I32)) for k in range(NY)] for u in used]
    start = []
    tables = []
    for turn in (1, -1):
        st = {}
        end = jnp.zeros((8, 128), I32)
        table = jnp.zeros((8, 128), I32)
        for p, d in ORDER:
            at = end
            if p == 1 and d == 0:
                at = jnp.maximum(at, SECOND)
            if d > 0:
                came = pltpu.roll(st[p, d - 1], turn % 8, 0)
                at = jnp.maximum(at, came + LAG)
            st[p, d] = at
            count = size[p] if d == 0 else pltpu.roll(size[p], (turn * d) % 8, 0)
            end = at + count
            spot = lane - at
            if d == 0:
                entry = jnp.zeros((8, 128), I32)
                for k in range(NY):
                    hit = (used[p][k] == 1) & (before[p][k] == spot)
                    entry = entry + jnp.where(hit, p * NY + k, 0)
            else:
                entry = OWN + came + spot
            table = jnp.where((lane >= at) & (lane < end), entry, table)
        start.append(st)
        tables.append(table)
    earlier = (owner_col == owner_row) & (
        lax.broadcasted_iota(I32, (32, 128), 0) < lax.broadcasted_iota(I32, (32, 128), 1)
    )
    slot = jnp.broadcast_to(jnp.sum(earlier.astype(I32), axis=0, keepdims=True), (8, 128))
    zb, yb = own >> 2, own & 3
    rank = jnp.zeros((8, 128), I32)
    for k in range(NY):
        line = jnp.sum((owner_col == (owner_row >> 2) * NY + k).astype(I32), axis=0, keepdims=True)
        line = jnp.broadcast_to(line, (8, 128))
        rank = rank + ((line > slot) & (yb > k)).astype(I32)
    found = []
    for way, turn in enumerate((1, -1)):
        hops = (turn * (z - zb)) & 7
        came_at = jnp.zeros((8, 128), I32)
        sender = (z - turn) & 7
        for p in range(SLOTS_DEV):
            for d in range(7):
                st = jnp.sum(jnp.where(row == sender, start[way][p, d], 0), axis=0, keepdims=True)
                came_at = jnp.where((hops == d + 1) & (slot == p), st + rank, came_at)
        found.append(jnp.minimum(came_at, STEPS - 1))
    here = (zb == z).astype(I32)
    mine = slot * NY + yb
    finds = jnp.where(row == 0, found[0], 0)
    finds = jnp.where(row == 1, found[1], finds)
    finds = jnp.where(row == 2, here, finds)
    finds = jnp.where(row == 3, mine, finds)
    finds = jnp.where(row == 4, zb, finds)
    finds = jnp.where(row == 5, yb, finds)
    finds = jnp.where(row == 6, slot, finds)
    held = jnp.sum((own == z * NY + y).astype(I32), axis=1, keepdims=True)
    return tables, finds, held[:1]


def main_kernel(
    grads, left, right, left_root, right_root, second, owner_row, owner_col,
    left_new, right_new, second_new, zout, nout, oout, lout, sout, finds_out,
    xb, lp, mixed, stack, ol, zland, pool, zst, yst, ynear, yopp,
    table_v, table_s, part, rk, ry, rz, tile,
    xsend, xrecv, osend, orecv, zsend, zrecv, nsend, nrecv, psend, precv,
    rsend, rrecv, sysend, syrecv, szsend, szrecv, lsem, outsem,
):
    z, y, x, c = me()
    rack = x * 2 + c
    xp, xm = dev(z, y, (x + 1) % NX, c), dev(z, y, (x + NX - 1) % NX, c)
    sibling = dev(z, y, x, 1 - c)
    ypeer = [None] + [dev(z, (y + k) % NY, x, c) for k in range(1, NY)]
    zpeer = [None] + [dev((z + k) % NZ, y, x, c) for k in range(1, NZ)]
    rpeer = [None] + [(z * NY + y, (rack + k) % 8) for k in range(1, 8)]
    yn = (ypeer[1], ypeer[3])
    zn = (zpeer[1], zpeer[7])

    barrier = pltpu.get_barrier_semaphore()
    peers = ypeer[1:] + zpeer[1:] + rpeer[1:]
    for p in peers:
        pl.semaphore_signal(barrier, inc=1, device_id=p, device_id_type=MESH)
    pl.semaphore_wait(barrier, len(peers))

    def source(w):
        return (grads, right_root)[w % 2].at[w // 2]

    def xrow(xx, lo, n):
        return pl.ds(pl.multiple_of((c * NX + xx) * ROWS + lo, 64), n)

    def x_copy(w, k):
        lo = (0, 64, 64, 0)[k] if k < 4 else (0, 64)[k - 4]
        if k < 4:
            src = source(w).at[lo : lo + 64]
            dst = xb.at[w, xrow(x, lo, 64)]
        else:
            frm = (x + NX - 1) % NX if k == 4 else (x + 1) % NX
            src = dst = xb.at[w, xrow(frm, lo, 64)]
        to = (xp, xp, xm, xm, xp, xm)[k]
        return rcopy(src, dst, xsend.at[w, k], xrecv.at[w, k], to)

    def core_copy(w):
        rows = xb.at[w, pl.ds(pl.multiple_of(c * 512, 512), 512)]
        return rcopy(rows, rows, xsend.at[w, 6], xrecv.at[w, 6], sibling)

    def x_own(w):
        for k in (0, 2, 1, 3):
            x_copy(w, k).start()
        xb[w, xrow(x, 0, ROWS), :] = source(w)[...]

    def x_forward(w):
        x_copy(w, 0).wait_recv()
        x_copy(w, 4).start()
        x_copy(w, 2).wait_recv()
        x_copy(w, 5).start()

    def x_rest(w):
        for k in (1, 3, 4, 5):
            x_copy(w, k).wait_recv()
        core_copy(w).start()

    def x_done(w):
        core_copy(w).wait_recv()

    def x_drain(w):
        for k in range(6):
            x_copy(w, k).wait_send()
        core_copy(w).wait_send()

    def mix(s):
        for k in range(8):
            to = (k % 2) * NX + k // 2
            lp[:, to * 128 : to * 128 + 128] = left_root[s, :, k * 128 : k * 128 + 128]
        for m in range(4):
            got = jnp.dot(lp[...], xb[2 * s, :, m * 256 : m * 256 + 256], preferred_element_type=F32)
            got = got.astype(BF)
            mixed[:, m * 128 : m * 128 + 128] = got[:, :128]
            mixed[:, 512 + m * 128 : 512 + m * 128 + 128] = got[:, 128:]

    def precondition(s):
        total = jnp.zeros((8, 128), F32)
        for m in range(4):
            got = jnp.dot(mixed[...], xb[2 * s + 1, :, m * 256 : m * 256 + 256], preferred_element_type=F32)
            got_b = got.astype(BF)
            stack[s, m * 256 : m * 256 + 128, :] = got_b[:, :128]
            stack[s, m * 256 + 128 : m * 256 + 256, :] = got_b[:, 128:]
            sq = got * got
            sq = sq[:, :128] + sq[:, 128:]
            total = total + jnp.sum(sq.reshape(16, 8, 128), axis=0)
        part[2 * s + 1] = total

    def factors(s, keep):
        for m in range(4):
            a, h = m // 2, m % 2
            outer = lax.dot_general(
                grads[s], xb[2 * s, m * 256 : m * 256 + 256, :], (((1,), (1,)), ((), ())),
                preferred_element_type=F32,
            )
            for i in range(2):
                col = ((2 * h + i) * 2 + a) * 128
                old = left[s, :, col : col + 128]
                old = old.astype(F32)
                new = 0.95 * old + 0.05 * outer[:, i * 128 : i * 128 + 128]
                left_new[s, :, col : col + 128] = jnp.where(keep, new, old).astype(BF)
        mine = xb[2 * s, :, pl.ds(pl.multiple_of(rack * 128, 128), 128)]
        for m in range(4):
            cols = slice(m * 256, m * 256 + 256)
            inner = lax.dot_general(
                mine, xb[2 * s, :, cols], (((0,), (0,)), ((), ())), preferred_element_type=F32
            )
            old = right[s, :, cols].astype(F32)
            new = 0.95 * old + 0.05 * inner
            right_new[s, :, cols] = jnp.where(keep, new, old).astype(BF)

    def graft(s, keep):
        def tile_rows(i, total):
            rows = pl.ds(pl.multiple_of(i * 16, 16), 16)
            g = grads[s, rows, :].astype(F32)
            old = second[s, rows, :].astype(F32)
            moment = 0.95 * old + 0.05 * g * g
            second_new[s, rows, :] = jnp.where(keep, moment, old).astype(BF)
            adam = g / (jnp.sqrt(moment) + 1e-8)
            return total + adam * adam

        total = lax.fori_loop(0, 8, tile_rows, jnp.zeros((16, WIDTH), F32))
        total = jnp.sum(total.reshape(2, 8, WIDTH), axis=0)
        acc = total[:, :128]
        for k in range(1, 8):
            acc = acc + total[:, k * 128 : k * 128 + 128]
        part[2 * s] = acc

    def quarter(k):
        return pl.ds(pl.multiple_of(FIRST_B + QUARTER * k, 16), QUARTER)

    def line_copy(s, k, i):
        to = (y + k) % NY
        rows = pl.ds(0, FIRST_B) if i == 0 else quarter((to + i - 1) % NY)
        return rcopy(
            stack.at[s, rows], ol.at[s * NY + y, rows], osend.at[s, k - 1, i], orecv.at[s, k - 1, i], ypeer[k]
        )

    def line_recv(s, k, i):
        frm = (y + NY - k) % NY
        rows = pl.ds(0, FIRST_B) if i == 0 else quarter((y + i - 1) % NY)
        return rcopy(
            stack.at[s, rows], ol.at[s * NY + frm, rows], osend.at[s, k - 1, i], orecv.at[s, k - 1, i], ypeer[k]
        )

    def line_first(s):
        for i in (0, 1):
            for k in (1, 3, 2):
                line_copy(s, k, i).start()
        ol[pl.ds(s * NY + y, 1)] = stack[s][None]

    def line_second(s):
        for i in (2, 3, 4):
            for k in (1, 3, 2):
                line_copy(s, k, i).start()

    def line_pool(s):
        for i in (0, 1):
            for k in (1, 3, 2):
                line_recv(s, k, i).wait_recv()
        for k in range(NY):
            e = s * NY + k
            for way in range(2):
                pool[way, e, :HALF_A] = ol[e, way * HALF_A : way * HALF_A + HALF_A, :]
                lo = pl.multiple_of(FIRST_B + QUARTER * y + way * HALF_B, 16)
                pool[way, e, HALF_A:] = ol[e, pl.ds(lo, HALF_B), :]

    def z_copy(way, t):
        return rcopy(
            zst.at[way, t % KEEP], zland.at[way, t], zsend.at[way, t % KEEP], zrecv.at[way, t], zn[way]
        )

    def n_copy(way, t):
        return rcopy(yst.at[t], ynear.at[way, t], nsend.at[way, t % KEEP], nrecv.at[way, t], yn[way])

    def p_copy(way, t):
        return rcopy(
            ynear.at[way, t, pl.ds(way * HALF_B, HALF_B)], yopp.at[way, t],
            psend.at[way, t % KEEP], precv.at[way, t], yn[way],
        )

    def z_send(t, again):
        for way in range(2):
            if again:
                z_copy(way, t - KEEP).wait_send()
            zst[way, t % KEEP] = pool[way, table_s[way, z, t]]
            z_copy(way, t).start()

    def z_take(t, again):
        for way in range(2):
            z_copy(way, t).wait_recv()
            pool[way, OWN + t] = zland[way, t]
            yst[t, way * HALF_B : way * HALF_B + HALF_B, :] = zland[way, t, HALF_A:, :]
        for way in range(2):
            if again:
                n_copy(way, t - KEEP).wait_send()
            n_copy(way, t).start()

    def y_take(t, again):
        for way in range(2):
            n_copy(way, t).wait_recv()
            if again:
                p_copy(way, t - KEEP).wait_send()
            p_copy(way, t).start()

    marks = sorted({0, LAG, LAG + LAG_Y, KEEP, KEEP + LAG, KEEP + LAG + LAG_Y, STEPS, STEPS + LAG, STEPS + LAG + LAG_Y})

    def steps(a, b):
        cuts = [a] + [k for k in marks if a < k < b] + [b]
        for lo, hi in zip(cuts[:-1], cuts[1:]):
            def body(t, _, lo=lo):
                if LAG <= lo < STEPS + LAG:
                    z_take(t - LAG, lo - LAG >= KEEP)
                if lo < STEPS:
                    z_send(t, lo >= KEEP)
                if LAG + LAG_Y <= lo < STEPS + LAG + LAG_Y:
                    y_take(t - LAG - LAG_Y, lo - LAG - LAG_Y >= KEEP)
                return 0

            lax.fori_loop(lo, hi, body, 0)

    def r_copy(k):
        return rcopy(tile.at[0], rk.at[k], rsend.at[k - 1], rrecv.at[k - 1], rpeer[k])

    def sy_copy(k):
        return rcopy(tile.at[1], ry.at[y], sysend.at[k - 1], syrecv.at[k - 1], ypeer[k])

    def sz_copy(k):
        return rcopy(ry, rz.at[z], szsend.at[k - 1], szrecv.at[k - 1], zpeer[k])

    sub = lax.broadcasted_iota(I32, (8, 128), 0)

    def scale_first():
        own = jnp.zeros((8, 128), F32)
        for i in range(4):
            whole = jnp.sum(jnp.sum(part[i], axis=0, keepdims=True), axis=1, keepdims=True)
            own = jnp.where(sub == i, jnp.broadcast_to(whole, (8, 128)), own)
        tile[0] = own
        rk[0] = own
        for k in range(1, 8):
            r_copy(k).start()

    def scale_second():
        for k in range(1, 8):
            r_copy(k).wait_recv()
        total = rk[0]
        for k in range(1, 8):
            total = total + rk[k]
        out = jnp.zeros((8, 128), F32)
        for s in range(2):
            value = jnp.sqrt(total[2 * s : 2 * s + 1]) / jnp.sqrt(total[2 * s + 1 : 2 * s + 2] + 1e-6)
            out = jnp.where(sub == s, jnp.broadcast_to(value, (8, 128)), out)
        tile[1] = out
        ry[pl.ds(y, 1)] = out[None]
        for k in range(1, 4):
            sy_copy(k).start()

    def sy_recv(k):
        frm = (y + NY - k) % NY
        return rcopy(tile.at[1], ry.at[frm], sysend.at[k - 1], syrecv.at[k - 1], ypeer[k])

    def sz_recv(k):
        frm = (z + NZ - k) % NZ
        return rcopy(ry, rz.at[frm], szsend.at[k - 1], szrecv.at[k - 1], zpeer[k])

    def scale_third():
        for k in range(1, 4):
            sy_recv(k).wait_recv()
        rz[pl.ds(z, 1)] = ry[...][None]
        for k in range(1, 8):
            sz_copy(k).start()

    x_own(0)
    tables, finds, held = schedule(owner_row[...], owner_col[...], z, y)
    for way in range(2):
        table_v[way] = tables[way]
    finds_out[...] = finds
    to_smem = pltpu.make_async_copy(table_v, table_s, lsem.at[0])
    to_smem.start()
    x_forward(0)
    x_own(1)
    graft(0, held > 0)
    graft(1, held > 1)
    x_rest(0)
    x_forward(1)
    x_own(2)
    x_done(0)
    mix(0)
    x_rest(1)
    x_forward(2)
    x_own(3)
    x_done(1)
    precondition(0)
    line_first(0)
    factors(0, held > 0)
    to_smem.wait()
    line_pool(0)
    steps(0, 2)
    line_second(0)
    x_rest(2)
    x_forward(3)
    steps(2, 4)
    x_done(2)
    mix(1)
    steps(4, 6)
    x_rest(3)
    steps(6, 8)
    x_done(3)
    precondition(1)
    line_first(1)
    scale_first()
    steps(8, SECOND)
    line_pool(1)
    steps(SECOND, SECOND + 3)
    line_second(1)
    scale_second()
    factors(1, held > 1)
    steps(SECOND + 3, SECOND + 8)
    scale_third()
    steps(SECOND + 8, STEPS + LAG + LAG_Y)

    def put(i, src, dst):
        return pltpu.make_async_copy(src, dst, outsem.at[i])

    puts = [put(0, zland, zout), put(1, ynear, nout)]
    for p in puts:
        p.start()
    for s in range(2):
        for i in (2, 3, 4):
            for k in (1, 3, 2):
                line_recv(s, k, i).wait_recv()
    more = [put(2, ol, lout)]
    more[0].start()
    for k in range(1, 8):
        sz_recv(k).wait_recv()
    more.append(put(3, rz, sout))
    more[1].start()
    for t in range(STEPS):
        for way in range(2):
            p_copy(way, t).wait_recv()
    more.append(put(4, yopp, oout))
    more[2].start()
    for w in range(4):
        x_drain(w)
    for s in range(2):
        for k in range(1, 4):
            for i in range(5):
                line_copy(s, k, i).wait_send()
    for t in range(STEPS - KEEP, STEPS):
        for way in range(2):
            z_copy(way, t).wait_send()
            n_copy(way, t).wait_send()
            p_copy(way, t).wait_send()
    for k in range(1, 8):
        r_copy(k).wait_send()
        sz_copy(k).wait_send()
    for k in range(1, 4):
        sy_copy(k).wait_send()
    for p in puts + more:
        p.wait()


def spread_kernel(finds, zp, near, opp, line, scales, out, zv, nv, ov, lv, sv, flat, rows_out, insem, outsem):
    _, y, _, _ = me()
    pairs = [(zp, zv), (near, nv), (opp, ov), (line, lv), (scales, sv)]
    loads = [pltpu.make_async_copy(a, b, insem.at[i]) for i, (a, b) in enumerate(pairs)]
    for k in loads:
        k.start()
    for k in loads:
        k.wait()

    def store(b, src):
        keep = b % 4
        scale = sv[finds[4, b], finds[5, b], pl.ds(finds[6, b], 1), :]

        @pl.when(b >= 4)
        def _():
            pltpu.make_async_copy(rows_out.at[keep], out.at[b - 4], outsem.at[keep]).wait()

        for col in range(8):
            part = src(col).astype(F32) * scale
            rows_out[keep, :, col * 128 : col * 128 + 128] = part.astype(BF)
        pltpu.make_async_copy(rows_out.at[keep], out.at[b], outsem.at[keep]).start()

    def one(b, _):
        tp, tm = finds[0, b], finds[1, b]

        @pl.when(finds[2, b] == 1)
        def _():
            e = finds[3, b]
            store(b, lambda col: lv[e, col * 128 : col * 128 + 128, :])

        @pl.when(finds[2, b] == 0)
        def _():
            flat[:HALF_A] = zv[0, tp, :HALF_A]
            flat[HALF_A : 2 * HALF_A] = zv[1, tm, :HALF_A]

            def quarter(q, plus, minus):
                lo = pl.multiple_of(FIRST_B + QUARTER * (q % NY), 16)
                flat[pl.ds(lo, HALF_B)] = plus
                flat[pl.ds(pl.multiple_of(lo + HALF_B, 16), HALF_B)] = minus

            quarter(y, zv[0, tp, HALF_A:], zv[1, tm, HALF_A:])
            quarter(y + NY - 1, nv[0, tp, :HALF_B], nv[0, tm, HALF_B:])
            quarter(y + 1, nv[1, tp, :HALF_B], nv[1, tm, HALF_B:])
            quarter(y + 2, ov[0, tp], ov[1, tm])
            store(b, lambda col: flat[col * 128 : col * 128 + 128])

        return 0

    lax.fori_loop(0, 32, one, 0)
    for b in range(28, 32):
        pltpu.make_async_copy(rows_out.at[b % 4], out.at[b], outsem.at[b % 4]).wait()


def on_device(grads, left, right, left_root, right_root, second, owner):
    owner_row = jnp.pad(owner, (0, 128 - owner.shape[0]), constant_values=-1).reshape(1, 128)
    owner_col = jnp.broadcast_to(owner[:, None], (32, 128))
    vmem, hbm = pl.BlockSpec(memory_space=pltpu.VMEM), pl.BlockSpec(memory_space=pl.ANY)
    shape = jax.ShapeDtypeStruct
    block = shape((SLOTS_DEV, ROWS, WIDTH), BF)
    z_shape, n_shape, o_shape = (2, STEPS, CHUNK, 128), (2, STEPS, QUARTER, 128), (2, STEPS, HALF_B, 128)
    l_shape, s_shape = (OWN, WIDTH, 128), (NZ, NY, 8, 128)
    dma = pltpu.SemaphoreType.DMA
    left_new, right_new, second_new, zp, near, opp, line, scales, finds = pl.pallas_call(
        main_kernel,
        out_shape=(
            block, block, block, shape(z_shape, BF), shape(n_shape, BF), shape(o_shape, BF), shape(l_shape, BF),
            shape(s_shape, F32), shape((8, 128), I32),
        ),
        in_specs=[vmem] * 8,
        out_specs=(vmem, vmem, vmem, hbm, hbm, hbm, hbm, hbm, vmem),
        scratch_shapes=[
            pltpu.VMEM((4, WIDTH, WIDTH), BF),
            pltpu.VMEM((ROWS, WIDTH), BF),
            pltpu.VMEM((ROWS, WIDTH), BF),
            pltpu.VMEM((SLOTS_DEV, WIDTH, 128), BF),
            pltpu.VMEM(l_shape, BF),
            pltpu.VMEM(z_shape, BF),
            pltpu.VMEM((2, OWN + STEPS, CHUNK, 128), BF),
            pltpu.VMEM((2, KEEP, CHUNK, 128), BF),
            pltpu.VMEM((STEPS, QUARTER, 128), BF),
            pltpu.VMEM(n_shape, BF),
            pltpu.VMEM(o_shape, BF),
            pltpu.VMEM((2, 8, 128), I32),
            pltpu.SMEM((2, 8, 128), I32),
            pltpu.VMEM((4, 8, 128), F32),
            pltpu.VMEM((8, 8, 128), F32),
            pltpu.VMEM((NY, 8, 128), F32),
            pltpu.VMEM(s_shape, F32),
            pltpu.VMEM((2, 8, 128), F32),
            dma((4, 7)), dma((4, 7)),
            dma((2, 3, 5)), dma((2, 3, 5)),
            dma((2, KEEP)), dma((2, STEPS)),
            dma((2, KEEP)), dma((2, STEPS)),
            dma((2, KEEP)), dma((2, STEPS)),
            dma((7,)), dma((7,)), dma((3,)), dma((3,)), dma((7,)), dma((7,)),
            dma((1,)), dma((5,)),
        ],
        compiler_params=pltpu.CompilerParams(
            collective_id=1, has_side_effects=True, vmem_limit_bytes=56 << 20
        ),
        name="shampoo",
    )(grads, left, right, left_root, right_root, second, owner_row, owner_col)
    directions = pl.pallas_call(
        spread_kernel,
        out_shape=shape((32, ROWS, WIDTH), BF),
        in_specs=[pl.BlockSpec(memory_space=pltpu.SMEM)] + [hbm] * 5,
        out_specs=hbm,
        scratch_shapes=[
            pltpu.VMEM(z_shape, BF), pltpu.VMEM(n_shape, BF), pltpu.VMEM(o_shape, BF), pltpu.VMEM(l_shape, BF),
            pltpu.VMEM(s_shape, F32),
            pltpu.VMEM((WIDTH, 128), BF),
            pltpu.VMEM((4, ROWS, WIDTH), BF),
            dma((5,)), dma((4,)),
        ],
        compiler_params=pltpu.CompilerParams(vmem_limit_bytes=48 << 20),
        name="spread",
    )(finds, zp, near, opp, line, scales)
    return (left_new, right_new, second_new, directions)


def solution(mesh):
    block = P("rep", "rack", None)
    return jax.shard_map(
        on_device,
        mesh=mesh,
        in_specs=(block,) * 6 + (P(),),
        out_specs=(block, block, block, P(None, "rack", None)),
        check_vma=False,
    )
```

```python
import functools

import jax
import jax.numpy as jnp
from jax import lax
from jax.experimental import pallas as pl
from jax.experimental.pallas import tpu as pltpu
from jax.sharding import PartitionSpec as P

MESH = pl.DeviceIdType.MESH
BF, F32, I32 = jnp.bfloat16, jnp.float32, jnp.int32

NX, NY, NZ = 4, 4, 8
ROWS, WIDTH, SLOTS_DEV = 128, 1024, 2
HALF_A = 192
QUARTER = 160
HALF_B = QUARTER // 2
FIRST_B = 2 * HALF_A
CHUNK = HALF_A + HALF_B
OWN = SLOTS_DEV * NY
LAG = 3
LAG_Y = 5
SECOND = 10
STEPS = 44
KEEP = 8
ORDER = (
    (0, 0), (0, 1), (0, 2), (1, 0), (0, 3), (1, 1), (0, 4), (1, 2), (0, 5), (1, 3), (0, 6), (1, 4), (1, 5), (1, 6),
)


def me():
    rep, rack = lax.axis_index("rep"), lax.axis_index("rack")
    return rep // NY, rep % NY, rack // 2, rack % 2


def dev(z, y, x, c):
    return (z * NY + y, x * 2 + c)


def rcopy(src, dst, send, recv, to):
    return pltpu.make_async_remote_copy(
        src_ref=src, dst_ref=dst, send_sem=send, recv_sem=recv, device_id=to, device_id_type=MESH
    )


def schedule(owner, z, y):
    row = lax.broadcasted_iota(I32, (8, 128), 0)
    lane = lax.broadcasted_iota(I32, (8, 128), 1)
    own = jnp.full((8, 128), -1, I32)
    owner_col = jnp.zeros((32, 128), I32)
    sub = lax.broadcasted_iota(I32, (32, 128), 0)
    for b in range(32):
        own = jnp.where(lane == b, owner[b], own)
        owner_col = jnp.where(sub == b, owner[b], owner_col)
    owner_row = own[:1]
    cnt = [
        jnp.broadcast_to(
            jnp.sum((own == row * NY + k).astype(I32), axis=1, keepdims=True), (8, 128)
        )
        for k in range(NY)
    ]
    used = [[(c > p).astype(I32) for c in cnt] for p in range(SLOTS_DEV)]
    size = [u[0] + u[1] + u[2] + u[3] for u in used]
    before = [[sum(u[:k], jnp.zeros((8, 128), I32)) for k in range(NY)] for u in used]
    start = []
    tables = []
    for turn in (1, -1):
        st = {}
        end = jnp.zeros((8, 128), I32)
        table = jnp.zeros((8, 128), I32)
        for p, d in ORDER:
            at = end
            if p == 1 and d == 0:
                at = jnp.maximum(at, SECOND)
            if d > 0:
                came = pltpu.roll(st[p, d - 1], turn % 8, 0)
                at = jnp.maximum(at, came + LAG)
            st[p, d] = at
            count = size[p] if d == 0 else pltpu.roll(size[p], (turn * d) % 8, 0)
            end = at + count
            spot = lane - at
            if d == 0:
                entry = jnp.zeros((8, 128), I32)
                for k in range(NY):
                    hit = (used[p][k] == 1) & (before[p][k] == spot)
                    entry = entry + jnp.where(hit, p * NY + k, 0)
            else:
                entry = OWN + came + spot
            table = jnp.where((lane >= at) & (lane < end), entry, table)
        start.append(st)
        tables.append(table)
    earlier = (owner_col == owner_row) & (
        lax.broadcasted_iota(I32, (32, 128), 0) < lax.broadcasted_iota(I32, (32, 128), 1)
    )
    slot = jnp.broadcast_to(jnp.sum(earlier.astype(I32), axis=0, keepdims=True), (8, 128))
    zb, yb = own >> 2, own & 3
    rank = jnp.zeros((8, 128), I32)
    for k in range(NY):
        line = jnp.sum((owner_col == (owner_row >> 2) * NY + k).astype(I32), axis=0, keepdims=True)
        line = jnp.broadcast_to(line, (8, 128))
        rank = rank + ((line > slot) & (yb > k)).astype(I32)
    found = []
    for way, turn in enumerate((1, -1)):
        hops = (turn * (z - zb)) & 7
        came_at = jnp.zeros((8, 128), I32)
        sender = (z - turn) & 7
        for p in range(SLOTS_DEV):
            for d in range(7):
                st = jnp.sum(jnp.where(row == sender, start[way][p, d], 0), axis=0, keepdims=True)
                came_at = jnp.where((hops == d + 1) & (slot == p), st + rank, came_at)
        found.append(jnp.minimum(came_at, STEPS - 1))
    here = (zb == z).astype(I32)
    mine = slot * NY + yb
    finds = jnp.where(row == 0, found[0], 0)
    finds = jnp.where(row == 1, found[1], finds)
    finds = jnp.where(row == 2, here, finds)
    finds = jnp.where(row == 3, mine, finds)
    finds = jnp.where(row == 4, zb, finds)
    finds = jnp.where(row == 5, yb, finds)
    finds = jnp.where(row == 6, slot, finds)
    held = jnp.sum((own == z * NY + y).astype(I32), axis=1, keepdims=True)
    return tables, finds, held[:1]


def main_kernel(
    grads_h, left_h, right_h, left_root_h, right_root_h, second_h, owner,
    left_o, right_o, second_o, zout, nout, oout, lout, sout, finds_o,
    grads, left, right, left_root, second, left_new, right_new, second_new, finds_out, xb, mixed, stack, ol, zland, pool, zst, yst, ynear, yopp,
    table_v, table_s, part, rk, ry, rz, tile,
    xsend, xrecv, osend, orecv, zsend, zrecv, nsend, nrecv, psend, precv,
    rsend, rrecv, sysend, syrecv, szsend, szrecv, lsem, insem, outsem,
):
    z, y, x, c = me()
    rack = x * 2 + c
    xp, xm = dev(z, y, (x + 1) % NX, c), dev(z, y, (x + NX - 1) % NX, c)
    sibling = dev(z, y, x, 1 - c)
    ypeer = [None] + [dev(z, (y + k) % NY, x, c) for k in range(1, NY)]
    zpeer = [None] + [dev((z + k) % NZ, y, x, c) for k in range(1, NZ)]
    rpeer = [None] + [(z * NY + y, (rack + k) % 8) for k in range(1, 8)]
    yn = (ypeer[1], ypeer[3])
    zn = (zpeer[1], zpeer[7])

    barrier = pltpu.get_barrier_semaphore()
    peers = ypeer[1:] + zpeer[1:] + rpeer[1:]
    for p in peers:
        pl.semaphore_signal(barrier, inc=1, device_id=p, device_id_type=MESH)
    pl.semaphore_wait(barrier, len(peers))

    after, two, prior = (x + 1) % NX, (x + 2) % NX, (x + 3) % NX

    def source(w):
        return (grads_h, right_root_h)[w % 2].at[w // 2]

    def brow(xx, cc, lo=0, n=ROWS):
        return pl.ds(pl.multiple_of((xx * 2 + cc) * ROWS + lo, 64), n)

    def bcol(xx):
        return pl.ds(pl.multiple_of(xx * 256, 256), 256)

    def x_copy(w, k):
        if w % 2 == 0:
            lo = (0, 64, 64, 0, 0, 64)[k]
            to = (xp, xp, xm, xm, xp, xm)[k]
            if k < 4:
                src, dst = source(w).at[lo : lo + 64], xb.at[w, brow(x, c, lo, 64)]
            else:
                src = dst = xb.at[w, brow(prior if k == 4 else after, c, lo, 64)]
        else:
            to = (xp, xp, xp, xm, xm, xm)[k]
            col = bcol((x, prior, two, x, after, after)[k])
            if k < 5:
                src, dst = source(w).at[:, col], xb.at[w, brow(x, c), col]
            else:
                src = dst = xb.at[w, brow(after, c), col]
        return rcopy(src, dst, xsend.at[w, k], xrecv.at[w, k], to)

    def core_copy(w, i):
        rows = brow((x, prior, after, two)[i], c)
        src = source(w) if i == 0 else xb.at[w, rows]
        return rcopy(src, xb.at[w, rows], xsend.at[w, 6 + i], xrecv.at[w, 6 + i], sibling)

    def own_copy(w):
        return pltpu.make_async_copy(source(w), xb.at[w, brow(x, c)], insem.at[w])

    def x_own(w):
        for k in ((0, 2, 1, 3), (3, 0, 4, 1, 2))[w % 2]:
            x_copy(w, k).start()
        core_copy(w, 0).start()
        own_copy(w).start()

    def x_forward(w):
        for k, on in (((0, 4), (2, 5)), ((3, 5),))[w % 2]:
            x_copy(w, k).wait_recv()
            x_copy(w, on).start()

    def x_rest(w):
        for i, ks in enumerate((((1,), (3,), (4, 5)), ((0, 1, 2), (4,), (5,)))[w % 2]):
            for k in ks:
                x_copy(w, k).wait_recv()
            core_copy(w, 1 + i).start()

    def x_held(w):
        own_copy(w).wait()
        core_copy(w, 0).wait_recv()

    def x_done(w):
        for i in range(1, 4):
            core_copy(w, i).wait_recv()

    def x_drain(w):
        for k in range(6):
            x_copy(w, k).wait_send()
        for i in range(4):
            core_copy(w, i).wait_send()

    def mix(s):
        for m in range(4):
            cols = slice(m * 256, m * 256 + 256)
            mixed[:, cols] = jnp.dot(left_root[s], xb[2 * s, :, cols], preferred_element_type=F32).astype(BF)

    def precondition(s, j):
        w = 2 * s + 1
        at = ((x, after, two, prior)[j]) * 256
        got = jnp.zeros((ROWS, 256), F32)
        for i in range(4):
            lhs = mixed[:, bcol((x + i) % NX)]
            here = i == 0 or (i, j) in ((3, 1), (3, 2), (3, 3), (1, 1), (1, 2), (2, 2))
            r, k = (i, j) if here else (j, i)
            block = xb[w, bcol((x + r) % NX), bcol((x + k) % NX)]
            got += lax.dot_general(
                lhs, block, (((1,), (0 if here else 1,)), ((), ())), preferred_element_type=F32
            )
        got_b = got.astype(BF)
        stack[s, pl.ds(pl.multiple_of(at, 256), 128), :] = got_b[:, :128]
        stack[s, pl.ds(pl.multiple_of(at + 128, 128), 128), :] = got_b[:, 128:]
        sq = got * got
        sq = jnp.sum((sq[:, :128] + sq[:, 128:]).reshape(16, 8, 128), axis=0)
        part[2 * s + 1] = sq if j == 0 else part[2 * s + 1] + sq

    def factors(s, keep):
        for m in range(4):
            cols = slice(m * 256, m * 256 + 256)
            outer = lax.dot_general(
                grads[s], xb[2 * s, cols, :], (((1,), (1,)), ((), ())), preferred_element_type=F32
            )
            old = left[s, :, cols].astype(F32)
            left_new[s, :, cols] = jnp.where(keep, 0.95 * old + 0.05 * outer, old).astype(BF)
        mine = xb[2 * s, :, pl.ds(pl.multiple_of(rack * 128, 128), 128)]
        for m in range(4):
            cols = slice(m * 256, m * 256 + 256)
            inner = lax.dot_general(
                mine, xb[2 * s, :, cols], (((0,), (0,)), ((), ())), preferred_element_type=F32
            )
            old = right[s, :, cols].astype(F32)
            new = 0.95 * old + 0.05 * inner
            right_new[s, :, cols] = jnp.where(keep, new, old).astype(BF)

    def graft(s, keep):
        def tile_rows(i, total):
            rows = pl.ds(pl.multiple_of(i * 16, 16), 16)
            g = grads[s, rows, :].astype(F32)
            old = second[s, rows, :].astype(F32)
            moment = 0.95 * old + 0.05 * g * g
            second_new[s, rows, :] = jnp.where(keep, moment, old).astype(BF)
            adam = g / (jnp.sqrt(moment) + 1e-8)
            return total + adam * adam

        total = lax.fori_loop(0, 8, tile_rows, jnp.zeros((16, WIDTH), F32))
        total = jnp.sum(total.reshape(2, 8, WIDTH), axis=0)
        acc = total[:, :128]
        for k in range(1, 8):
            acc = acc + total[:, k * 128 : k * 128 + 128]
        part[2 * s] = acc

    def quarter(k):
        return pl.ds(pl.multiple_of(FIRST_B + QUARTER * k, 16), QUARTER)

    def line_copy(s, k, i):
        to = (y + k) % NY
        rows = pl.ds(0, FIRST_B) if i == 0 else quarter((to + i - 1) % NY)
        return rcopy(
            stack.at[s, rows], ol.at[s * NY + y, rows], osend.at[s, k - 1, i], orecv.at[s, k - 1, i], ypeer[k]
        )

    def line_recv(s, k, i):
        frm = (y + NY - k) % NY
        rows = pl.ds(0, FIRST_B) if i == 0 else quarter((y + i - 1) % NY)
        return rcopy(
            stack.at[s, rows], ol.at[s * NY + frm, rows], osend.at[s, k - 1, i], orecv.at[s, k - 1, i], ypeer[k]
        )

    def line_first(s):
        for i in (0, 1):
            for k in (1, 3, 2):
                line_copy(s, k, i).start()
        ol[pl.ds(s * NY + y, 1)] = stack[s][None]

    def line_second(s):
        for i in (2, 3, 4):
            for k in (1, 3, 2):
                line_copy(s, k, i).start()

    def line_pool(s):
        for i in (0, 1):
            for k in (1, 3, 2):
                line_recv(s, k, i).wait_recv()
        for k in range(NY):
            e = s * NY + k
            for way in range(2):
                pool[way, e, :HALF_A] = ol[e, way * HALF_A : way * HALF_A + HALF_A, :]
                lo = pl.multiple_of(FIRST_B + QUARTER * y + way * HALF_B, 16)
                pool[way, e, HALF_A:] = ol[e, pl.ds(lo, HALF_B), :]

    def z_copy(way, t):
        return rcopy(
            zst.at[way, t % KEEP], zland.at[way, t], zsend.at[way, t % KEEP], zrecv.at[way, t], zn[way]
        )

    def n_copy(way, t):
        return rcopy(yst.at[t], ynear.at[way, t], nsend.at[way, t % KEEP], nrecv.at[way, t], yn[way])

    def p_copy(way, t):
        return rcopy(
            ynear.at[way, t, pl.ds(way * HALF_B, HALF_B)], yopp.at[way, t],
            psend.at[way, t % KEEP], precv.at[way, t], yn[way],
        )

    def z_send(t, again):
        for way in range(2):
            if again:
                z_copy(way, t - KEEP).wait_send()
            zst[way, t % KEEP] = pool[way, table_s[way, z, t]]
            z_copy(way, t).start()

    def z_take(t):
        for way in range(2):
            z_copy(way, t).wait_recv()
            pool[way, OWN + t] = zland[way, t]

    def y_send(t, again):
        for way in range(2):
            yst[t, way * HALF_B : way * HALF_B + HALF_B, :] = zland[way, t, HALF_A:, :]
        for way in range(2):
            if again:
                n_copy(way, t - KEEP).wait_send()
            n_copy(way, t).start()

    def y_take(t, again):
        for way in range(2):
            n_copy(way, t).wait_recv()
            if again:
                p_copy(way, t - KEEP).wait_send()
            p_copy(way, t).start()

    marks = sorted({0, LAG, LAG + LAG_Y, KEEP, KEEP + LAG, KEEP + LAG + LAG_Y, STEPS, STEPS + LAG, STEPS + LAG + LAG_Y})

    def steps(a, b):
        cuts = [a] + [k for k in marks if a < k < b] + [b]
        for lo, hi in zip(cuts[:-1], cuts[1:]):
            def body(t, _, lo=lo):
                if LAG <= lo < STEPS + LAG:
                    z_take(t - LAG)
                if lo < STEPS:
                    z_send(t, lo >= KEEP)
                if LAG <= lo < STEPS + LAG:
                    y_send(t - LAG, lo - LAG >= KEEP)
                if LAG + LAG_Y <= lo < STEPS + LAG + LAG_Y:
                    y_take(t - LAG - LAG_Y, lo - LAG - LAG_Y >= KEEP)
                return 0

            lax.fori_loop(lo, hi, body, 0)

    def r_copy(k):
        return rcopy(tile.at[0], rk.at[k], rsend.at[k - 1], rrecv.at[k - 1], rpeer[k])

    def sy_copy(k):
        return rcopy(tile.at[1], ry.at[y], sysend.at[k - 1], syrecv.at[k - 1], ypeer[k])

    def sz_copy(k):
        return rcopy(ry, rz.at[z], szsend.at[k - 1], szrecv.at[k - 1], zpeer[k])

    sub = lax.broadcasted_iota(I32, (8, 128), 0)

    def scale_first():
        own = jnp.zeros((8, 128), F32)
        for i in range(4):
            whole = jnp.sum(jnp.sum(part[i], axis=0, keepdims=True), axis=1, keepdims=True)
            own = jnp.where(sub == i, jnp.broadcast_to(whole, (8, 128)), own)
        tile[0] = own
        rk[0] = own
        for k in range(1, 8):
            r_copy(k).start()

    def scale_second():
        for k in range(1, 8):
            r_copy(k).wait_recv()
        total = rk[0]
        for k in range(1, 8):
            total = total + rk[k]
        out = jnp.zeros((8, 128), F32)
        for s in range(2):
            value = jnp.sqrt(total[2 * s : 2 * s + 1]) / jnp.sqrt(total[2 * s + 1 : 2 * s + 2] + 1e-6)
            out = jnp.where(sub == s, jnp.broadcast_to(value, (8, 128)), out)
        tile[1] = out
        ry[pl.ds(y, 1)] = out[None]
        for k in range(1, 4):
            sy_copy(k).start()

    def sy_recv(k):
        frm = (y + NY - k) % NY
        return rcopy(tile.at[1], ry.at[frm], sysend.at[k - 1], syrecv.at[k - 1], ypeer[k])

    def sz_recv(k):
        frm = (z + NZ - k) % NZ
        return rcopy(ry, rz.at[frm], szsend.at[k - 1], szrecv.at[k - 1], zpeer[k])

    def scale_third():
        for k in range(1, 4):
            sy_recv(k).wait_recv()
        rz[pl.ds(z, 1)] = ry[...][None]
        for k in range(1, 8):
            sz_copy(k).start()

    def put(i, src, dst):
        copy = pltpu.make_async_copy(src, dst, outsem.at[i])
        copy.start()
        puts.append(copy)

    def put_steps(lo, hi, i):
        put(i, zland.at[:, lo:hi], zout.at[:, lo:hi])

    puts = []
    x_own(0)
    loads = [
        pltpu.make_async_copy(src, dst, insem.at[4 + i])
        for i, (src, dst) in enumerate(
            [(grads_h, grads), (left_root_h, left_root), (second_h, second), (left_h, left), (right_h, right)]
        )
    ]
    for k in loads:
        k.start()
    tables, finds, held = schedule(owner, z, y)
    for way in range(2):
        table_v[way] = tables[way]
    finds_out[...] = finds
    to_smem = pltpu.make_async_copy(table_v, table_s, lsem.at[0])
    to_smem.start()
    x_forward(0)
    x_own(1)
    for k in loads:
        k.wait()
    put(0, finds_out, finds_o)
    graft(0, held > 0)
    graft(1, held > 1)
    put(1, second_new, second_o)
    x_rest(0)
    x_forward(1)
    x_own(2)
    x_held(0)
    x_done(0)
    mix(0)
    x_held(1)
    precondition(0, 0)
    x_rest(1)
    x_forward(2)
    x_own(3)
    x_done(1)
    for j in (3, 1, 2):
        precondition(0, j)
    line_first(0)
    factors(0, held > 0)
    to_smem.wait()
    line_pool(0)
    steps(0, 1)
    line_second(0)
    x_rest(2)
    x_forward(3)
    steps(1, 2)
    x_held(2)
    x_done(2)
    mix(1)
    x_held(3)
    precondition(1, 0)
    steps(2, 4)
    x_rest(3)
    steps(4, 6)
    x_done(3)
    for j in (3, 1, 2):
        precondition(1, j)
    line_first(1)
    scale_first()
    steps(6, SECOND)
    line_pool(1)
    steps(SECOND, SECOND + 3)
    line_second(1)
    scale_second()
    factors(1, held > 1)
    put(2, left_new, left_o)
    put(3, right_new, right_o)
    steps(SECOND + 3, SECOND + 8)
    put_steps(0, SECOND + 5, 4)
    scale_third()
    steps(SECOND + 8, SECOND + 18)
    put_steps(SECOND + 5, SECOND + 14, 5)
    put(6, ynear.at[:, : SECOND + 9], nout.at[:, : SECOND + 9])
    for s in range(2):
        for i in (2, 3, 4):
            for k in (1, 3, 2):
                line_recv(s, k, i).wait_recv()
    put(7, ol, lout)
    for k in range(1, 8):
        sz_recv(k).wait_recv()
    put(8, rz, sout)
    steps(SECOND + 18, STEPS)
    put_steps(SECOND + 14, STEPS - LAG, 9)
    steps(STEPS, STEPS + LAG)
    put_steps(STEPS - LAG, STEPS, 10)
    steps(STEPS + LAG, STEPS + LAG + LAG_Y)
    put(11, ynear.at[:, SECOND + 9 :], nout.at[:, SECOND + 9 :])
    for t in range(STEPS):
        for way in range(2):
            p_copy(way, t).wait_recv()
    put(12, yopp, oout)
    for w in range(4):
        x_drain(w)
    for s in range(2):
        for k in range(1, 4):
            for i in range(5):
                line_copy(s, k, i).wait_send()
    for t in range(STEPS - KEEP, STEPS):
        for way in range(2):
            z_copy(way, t).wait_send()
            n_copy(way, t).wait_send()
            p_copy(way, t).wait_send()
    for k in range(1, 8):
        r_copy(k).wait_send()
        sz_copy(k).wait_send()
    for k in range(1, 4):
        sy_copy(k).wait_send()
    for p in puts:
        p.wait()


def spread_kernel(
    finds, zp, near, opp, line, scales, left, right, second, out, left_new, right_new, second_new,
    zv, nv, ov, lv, sv, rows_out, held, insem, outsem,
):
    _, y, _, _ = me()
    pairs = [(scales, sv), (line, lv), (zp, zv), (near, nv), (opp, ov)]
    pairs += [(left, held.at[0]), (right, held.at[1]), (second, held.at[2])]
    moves = [pltpu.make_async_copy(a, b, insem.at[i]) for i, (a, b) in enumerate(pairs)]
    for k in moves:
        k.start()
    for k in moves[:5]:
        k.wait()
    for i, ref in enumerate((left_new, right_new, second_new)):
        moves[5 + i].wait()
        moves[5 + i] = pltpu.make_async_copy(held.at[i], ref, insem.at[5 + i])
        moves[5 + i].start()

    def back(b):
        return pltpu.make_async_copy(rows_out.at[b % 4], out.at[b], outsem.at[b % 4])

    def store(b, pieces):
        @pl.when(b >= 4)
        def _():
            back(b - 4).wait()

        scale = sv[finds[4, b], finds[5, b], pl.ds(finds[6, b], 1), :]
        tile = 0
        for count, get in pieces:
            for i in range(count):
                r, col = tile % 8 * 16, tile // 8 * 128
                part = get(i * 16).astype(F32) * scale
                rows_out[b % 4, r : r + 16, col : col + 128] = part.astype(BF)
                tile += 1
        back(b).start()

    def one(b, yy):
        tp, tm = finds[0, b], finds[1, b]

        @pl.when(finds[2, b] == 1)
        def _():
            e = finds[3, b]
            store(b, [(64, lambda lo: lv[e, lo : lo + 16, :])])

        @pl.when(finds[2, b] == 0)
        def _():
            def tiles(ref, lead, lo, n):
                return (n // 16, lambda at: ref[(*lead, slice(lo + at, lo + at + 16))])

            quarters = {
                yy: (tiles(zv, (0, tp), HALF_A, HALF_B), tiles(zv, (1, tm), HALF_A, HALF_B)),
                (yy + 3) % NY: (tiles(nv, (0, tp), 0, HALF_B), tiles(nv, (0, tm), HALF_B, HALF_B)),
                (yy + 1) % NY: (tiles(nv, (1, tp), 0, HALF_B), tiles(nv, (1, tm), HALF_B, HALF_B)),
                (yy + 2) % NY: (tiles(ov, (0, tp), 0, HALF_B), tiles(ov, (1, tm), 0, HALF_B)),
            }
            pieces = [tiles(zv, (0, tp), 0, HALF_A), tiles(zv, (1, tm), 0, HALF_A)]
            for q in range(NY):
                pieces += quarters[q]
            store(b, pieces)

    for yy in range(NY):

        @pl.when(y == yy)
        def _(yy=yy):
            def body(b, _):
                one(b, yy)
                return 0

            lax.fori_loop(0, 32, body, 0)

    for b in range(28, 32):
        back(b).wait()
    for k in moves[5:]:
        k.wait()


def on_device(grads, left, right, left_root, right_root, second, owner):
    smem, hbm = pl.BlockSpec(memory_space=pltpu.SMEM), pl.BlockSpec(memory_space=pl.ANY)
    shape = jax.ShapeDtypeStruct
    b_shape = (SLOTS_DEV, ROWS, WIDTH)
    block = shape(b_shape, BF)
    z_shape, n_shape, o_shape = (2, STEPS, CHUNK, 128), (2, STEPS, QUARTER, 128), (2, STEPS, HALF_B, 128)
    l_shape, s_shape = (OWN, WIDTH, 128), (NZ, NY, 8, 128)
    dma = pltpu.SemaphoreType.DMA
    left_new, right_new, second_new, zp, near, opp, line, scales, finds = pl.pallas_call(
        main_kernel,
        out_shape=(
            block, block, block, shape(z_shape, BF), shape(n_shape, BF), shape(o_shape, BF), shape(l_shape, BF),
            shape(s_shape, F32), shape((8, 128), I32),
        ),
        in_specs=[hbm] * 6 + [smem],
        out_specs=(hbm,) * 9,
        scratch_shapes=[pltpu.VMEM(b_shape, BF)] * 8
        + [
            pltpu.VMEM((8, 128), I32),
            pltpu.VMEM((4, WIDTH, WIDTH), BF),
            pltpu.VMEM((ROWS, WIDTH), BF),
            pltpu.VMEM((SLOTS_DEV, WIDTH, 128), BF),
            pltpu.VMEM(l_shape, BF),
            pltpu.VMEM(z_shape, BF),
            pltpu.VMEM((2, OWN + STEPS, CHUNK, 128), BF),
            pltpu.VMEM((2, KEEP, CHUNK, 128), BF),
            pltpu.VMEM((STEPS, QUARTER, 128), BF),
            pltpu.VMEM(n_shape, BF),
            pltpu.VMEM(o_shape, BF),
            pltpu.VMEM((2, 8, 128), I32),
            pltpu.SMEM((2, 8, 128), I32),
            pltpu.VMEM((4, 8, 128), F32),
            pltpu.VMEM((8, 8, 128), F32),
            pltpu.VMEM((NY, 8, 128), F32),
            pltpu.VMEM(s_shape, F32),
            pltpu.VMEM((2, 8, 128), F32),
            dma((4, 10)), dma((4, 10)),
            dma((2, 3, 5)), dma((2, 3, 5)),
            dma((2, KEEP)), dma((2, STEPS)),
            dma((2, KEEP)), dma((2, STEPS)),
            dma((2, KEEP)), dma((2, STEPS)),
            dma((7,)), dma((7,)), dma((3,)), dma((3,)), dma((7,)), dma((7,)),
            dma((1,)), dma((9,)), dma((13,)),
        ],
        compiler_params=pltpu.CompilerParams(
            collective_id=1, has_side_effects=True, vmem_limit_bytes=60 << 20
        ),
        name="shampoo",
    )(grads, left, right, left_root, right_root, second, owner)
    directions, left_new, right_new, second_new = pl.pallas_call(
        spread_kernel,
        out_shape=(shape((32, ROWS, WIDTH), BF), block, block, block),
        in_specs=[smem] + [hbm] * 8,
        out_specs=(hbm,) * 4,
        scratch_shapes=[
            pltpu.VMEM(z_shape, BF), pltpu.VMEM(n_shape, BF), pltpu.VMEM(o_shape, BF), pltpu.VMEM(l_shape, BF),
            pltpu.VMEM(s_shape, F32),
            pltpu.VMEM((4, ROWS, WIDTH), BF),
            pltpu.VMEM((3, *b_shape), BF),
            dma((8,)), dma((4,)),
        ],
        compiler_params=pltpu.CompilerParams(vmem_limit_bytes=60 << 20),
        name="spread",
    )(finds, zp, near, opp, line, scales, left_new, right_new, second_new)
    return (left_new, right_new, second_new, directions)


def solution(mesh):
    block = P("rep", "rack", None)
    return jax.shard_map(
        on_device,
        mesh=mesh,
        in_specs=(block,) * 6 + (P(),),
        out_specs=(block, block, block, P(None, "rack", None)),
        check_vma=False,
    )
```

```python
import functools

import jax
import jax.numpy as jnp
from jax import lax
from jax.experimental import pallas as pl
from jax.experimental.pallas import tpu as pltpu
from jax.sharding import PartitionSpec as P

MESH = pl.DeviceIdType.MESH
BF, F32, I32 = jnp.bfloat16, jnp.float32, jnp.int32

NX, NY, NZ = 4, 4, 8
ROWS, WIDTH, SLOTS_DEV = 128, 1024, 2
PLACE = (0, 3, 1, 2)
HALF_A = 192
QUARTER = 160
HALF_B = QUARTER // 2
FIRST_B = 2 * HALF_A
CHUNK = HALF_A + HALF_B
OWN = SLOTS_DEV * NY
LAG = 3
LAG_Y = 5
SECOND = 10
STEPS = 44
DIRECT = STEPS - 6
LAG_O = 3
KEEP_Y = 16
KEEP = 8
ORDER = (
    (0, 0), (0, 1), (0, 2), (1, 0), (0, 3), (1, 1), (0, 4), (1, 2), (0, 5), (1, 3), (0, 6), (1, 4), (1, 5), (1, 6),
)


def me():
    rep, rack = lax.axis_index("rep"), lax.axis_index("rack")
    return rep // NY, rep % NY, rack // 2, rack % 2


def dev(z, y, x, c):
    return (z * NY + y, x * 2 + c)


def rcopy(src, dst, send, recv, to):
    return pltpu.make_async_remote_copy(
        src_ref=src, dst_ref=dst, send_sem=send, recv_sem=recv, device_id=to, device_id_type=MESH
    )


def schedule(owner, z, y):
    row = lax.broadcasted_iota(I32, (8, 128), 0)
    lane = lax.broadcasted_iota(I32, (8, 128), 1)
    own = jnp.full((8, 128), -1, I32)
    owner_col = jnp.zeros((32, 128), I32)
    sub = lax.broadcasted_iota(I32, (32, 128), 0)
    for b in range(32):
        own = jnp.where(lane == b, owner[b], own)
        owner_col = jnp.where(sub == b, owner[b], owner_col)
    owner_row = own[:1]
    cnt = [
        jnp.broadcast_to(
            jnp.sum((own == row * NY + k).astype(I32), axis=1, keepdims=True), (8, 128)
        )
        for k in range(NY)
    ]
    used = [[(c > p).astype(I32) for c in cnt] for p in range(SLOTS_DEV)]
    size = [u[0] + u[1] + u[2] + u[3] for u in used]
    before = [[sum(u[:k], jnp.zeros((8, 128), I32)) for k in range(NY)] for u in used]
    start = []
    tables = []
    for turn in (1, -1):
        st = {}
        end = jnp.zeros((8, 128), I32)
        table = jnp.zeros((8, 128), I32)
        for p, d in ORDER:
            at = end
            if p == 1 and d == 0:
                at = jnp.maximum(at, SECOND)
            if d > 0:
                came = pltpu.roll(st[p, d - 1], turn % 8, 0)
                at = jnp.maximum(at, came + LAG)
            st[p, d] = at
            count = size[p] if d == 0 else pltpu.roll(size[p], (turn * d) % 8, 0)
            end = at + count
            spot = lane - at
            if d == 0:
                entry = jnp.zeros((8, 128), I32)
                for k in range(NY):
                    hit = (used[p][k] == 1) & (before[p][k] == spot)
                    entry = entry + jnp.where(hit, p * NY + k, 0)
            else:
                entry = OWN + came + spot
            table = jnp.where((lane >= at) & (lane < end), entry, table)
        start.append(st)
        tables.append(table)
    earlier = (owner_col == owner_row) & (
        lax.broadcasted_iota(I32, (32, 128), 0) < lax.broadcasted_iota(I32, (32, 128), 1)
    )
    slot = jnp.broadcast_to(jnp.sum(earlier.astype(I32), axis=0, keepdims=True), (8, 128))
    zb, yb = own >> 2, own & 3
    rank = jnp.zeros((8, 128), I32)
    for k in range(NY):
        line = jnp.sum((owner_col == (owner_row >> 2) * NY + k).astype(I32), axis=0, keepdims=True)
        line = jnp.broadcast_to(line, (8, 128))
        rank = rank + ((line > slot) & (yb > k)).astype(I32)
    here = zb == z
    found = []
    for way, turn in enumerate((1, -1)):
        hops = (turn * (z - zb)) & 7
        came_at = jnp.zeros((8, 128), I32)
        sender = (z - turn) & 7
        for p in range(SLOTS_DEV):
            for d in range(7):
                st = jnp.sum(jnp.where(row == sender, start[way][p, d], 0), axis=0, keepdims=True)
                came_at = jnp.where((hops == d + 1) & (slot == p), st + rank, came_at)
        found.append(jnp.where(here, slot * NY + yb, OWN + came_at))
    finds = jnp.where(row == 0, found[0], 0)
    finds = jnp.where(row == 1, found[1], finds)
    finds = jnp.where(row == 2, own, finds)
    finds = jnp.where(row == 3, slot, finds)
    held = jnp.sum((own == z * NY + y).astype(I32), axis=1, keepdims=True)
    return tables, finds, held[:1]


def main_kernel(
    grads_h, left_h, right_h, left_root_h, right_root_h, second_h, owner,
    left_o, right_o, second_o, blocks_o, sout, finds_o,
    grads, left, right, left_root, second, left_new, right_new, second_new, finds_out, xb, mixed, stack, ol, zland, pool, zst, yst, ynear, yopp, rows_out,
    table_v, table_s, part, rk, ry, rz, tile,
    xsend, xrecv, osend, orecv, zsend, zrecv, nsend, nrecv, psend, precv,
    rsend, rrecv, sysend, syrecv, szsend, szrecv, lsem, insem, outsem, blocksem,
):
    z, y, x, c = me()
    rack = x * 2 + c
    xp, xm = dev(z, y, (x + 1) % NX, c), dev(z, y, (x + NX - 1) % NX, c)
    sibling = dev(z, y, x, 1 - c)
    ypeer = [None] + [dev(z, (y + k) % NY, x, c) for k in range(1, NY)]
    zpeer = [None] + [dev((z + k) % NZ, y, x, c) for k in range(1, NZ)]
    rpeer = [None] + [(z * NY + y, (rack + k) % 8) for k in range(1, 8)]
    yn = (ypeer[1], ypeer[3])
    zn = (zpeer[1], zpeer[7])

    barrier = pltpu.get_barrier_semaphore()
    peers = ypeer[1:] + zpeer[1:] + rpeer[1:]
    for p in peers:
        pl.semaphore_signal(barrier, inc=1, device_id=p, device_id_type=MESH)
    pl.semaphore_wait(barrier, len(peers))

    after, two, prior = (x + 1) % NX, (x + 2) % NX, (x + 3) % NX

    def source(w):
        return (grads_h, right_root_h)[w % 2].at[w // 2]

    def brow(xx, cc, lo=0, n=ROWS):
        return pl.ds(pl.multiple_of((xx * 2 + cc) * ROWS + lo, 64), n)

    def bcol(xx):
        return pl.ds(pl.multiple_of(xx * 256, 256), 256)

    def x_copy(w, k):
        if w % 2 == 0:
            lo = (0, 64, 64, 0, 0, 64)[k]
            to = (xp, xp, xm, xm, xp, xm)[k]
            if k < 4:
                src, dst = source(w).at[lo : lo + 64], xb.at[w, brow(x, c, lo, 64)]
            else:
                src = dst = xb.at[w, brow(prior if k == 4 else after, c, lo, 64)]
        else:
            to = (xp, xp, xp, xm, xm, xm)[k]
            col = bcol((x, prior, two, x, after, after)[k])
            if k < 5:
                src, dst = source(w).at[:, col], xb.at[w, brow(x, c), col]
            else:
                src = dst = xb.at[w, brow(after, c), col]
        return rcopy(src, dst, xsend.at[w, k], xrecv.at[w, k], to)

    def core_copy(w, i):
        rows = brow((x, prior, after, two)[i], c)
        src = source(w) if i == 0 else xb.at[w, rows]
        return rcopy(src, xb.at[w, rows], xsend.at[w, 6 + i], xrecv.at[w, 6 + i], sibling)

    def own_copy(w):
        return pltpu.make_async_copy(source(w), xb.at[w, brow(x, c)], insem.at[w])

    def x_own(w):
        for k in ((0, 2, 1, 3), (3, 0, 4, 1, 2))[w % 2]:
            x_copy(w, k).start()
        core_copy(w, 0).start()
        own_copy(w).start()

    def x_forward(w):
        for k, on in (((0, 4), (2, 5)), ((3, 5),))[w % 2]:
            x_copy(w, k).wait_recv()
            x_copy(w, on).start()

    def x_rest(w):
        for i, ks in enumerate((((1,), (3,), (4, 5)), ((0, 1, 2), (4,), (5,)))[w % 2]):
            for k in ks:
                x_copy(w, k).wait_recv()
            core_copy(w, 1 + i).start()

    def x_held(w):
        own_copy(w).wait()
        core_copy(w, 0).wait_recv()

    def x_done(w):
        for i in range(1, 4):
            core_copy(w, i).wait_recv()

    def x_drain(w):
        for k in range(6):
            x_copy(w, k).wait_send()
        for i in range(4):
            core_copy(w, i).wait_send()

    def mix(s):
        for m in range(4):
            cols = slice(m * 256, m * 256 + 256)
            mixed[:, cols] = jnp.dot(left_root[s], xb[2 * s, :, cols], preferred_element_type=F32).astype(BF)

    def precondition(s, j):
        w = 2 * s + 1
        at = PLACE.index(j) * 256
        got = jnp.zeros((ROWS, 256), F32)
        for i in range(4):
            lhs = mixed[:, bcol((x + i) % NX)]
            here = i == 0 or (i, j) in ((3, 1), (3, 2), (3, 3), (1, 1), (1, 2), (2, 2))
            r, k = (i, j) if here else (j, i)
            block = xb[w, bcol((x + r) % NX), bcol((x + k) % NX)]
            got += lax.dot_general(
                lhs, block, (((1,), (0 if here else 1,)), ((), ())), preferred_element_type=F32
            )
        got_b = got.astype(BF)
        stack[s, at : at + 128, :] = got_b[:, :128]
        stack[s, at + 128 : at + 256, :] = got_b[:, 128:]
        sq = got * got
        sq = jnp.sum((sq[:, :128] + sq[:, 128:]).reshape(16, 8, 128), axis=0)
        part[2 * s + 1] = sq if j == 0 else part[2 * s + 1] + sq

    def factors(s, keep):
        for m in range(4):
            cols = slice(m * 256, m * 256 + 256)
            outer = lax.dot_general(
                grads[s], xb[2 * s, cols, :], (((1,), (1,)), ((), ())), preferred_element_type=F32
            )
            old = left[s, :, cols].astype(F32)
            left_new[s, :, cols] = jnp.where(keep, 0.95 * old + 0.05 * outer, old).astype(BF)
        mine = xb[2 * s, :, pl.ds(pl.multiple_of(rack * 128, 128), 128)]
        for m in range(4):
            cols = slice(m * 256, m * 256 + 256)
            inner = lax.dot_general(
                mine, xb[2 * s, :, cols], (((0,), (0,)), ((), ())), preferred_element_type=F32
            )
            old = right[s, :, cols].astype(F32)
            new = 0.95 * old + 0.05 * inner
            right_new[s, :, cols] = jnp.where(keep, new, old).astype(BF)

    def graft(s, keep):
        def tile_rows(i, total):
            rows = pl.ds(pl.multiple_of(i * 16, 16), 16)
            g = grads[s, rows, :].astype(F32)
            old = second[s, rows, :].astype(F32)
            moment = 0.95 * old + 0.05 * g * g
            second_new[s, rows, :] = jnp.where(keep, moment, old).astype(BF)
            adam = g / (jnp.sqrt(moment) + 1e-8)
            return total + adam * adam

        total = lax.fori_loop(0, 8, tile_rows, jnp.zeros((16, WIDTH), F32))
        total = jnp.sum(total.reshape(2, 8, WIDTH), axis=0)
        acc = total[:, :128]
        for k in range(1, 8):
            acc = acc + total[:, k * 128 : k * 128 + 128]
        part[2 * s] = acc

    def quarter(k):
        return pl.ds(pl.multiple_of(FIRST_B + QUARTER * k, 16), QUARTER)

    def line_part(s, k, i, sender, receiver):
        if i < 2:
            rows = pl.ds(0, 256) if i == 0 else pl.ds(256, FIRST_B - 256)
        else:
            rows = quarter((receiver + i - 2) % NY)
        return rcopy(
            stack.at[s, rows], ol.at[s * NY + sender, rows], osend.at[s, k - 1, i], orecv.at[s, k - 1, i], ypeer[k]
        )

    def line_copy(s, k, i):
        return line_part(s, k, i, y, (y + k) % NY)

    def line_recv(s, k, i):
        return line_part(s, k, i, (y + NY - k) % NY, y)

    def line_send(s, parts):
        for i in parts:
            for k in (1, 3, 2):
                line_copy(s, k, i).start()

    def line_pool(s):
        ol[pl.ds(s * NY + y, 1)] = stack[s][None]
        for i in (0, 1, 2):
            for k in (1, 3, 2):
                line_recv(s, k, i).wait_recv()
        for k in range(NY):
            e = s * NY + k
            for way in range(2):
                pool[way, e, :HALF_A] = ol[e, way * HALF_A : way * HALF_A + HALF_A, :]
                lo = pl.multiple_of(FIRST_B + QUARTER * y + way * HALF_B, 16)
                pool[way, e, HALF_A:] = ol[e, pl.ds(lo, HALF_B), :]

    def line_rest(s):
        for i in (3, 4, 5):
            for k in (1, 3, 2):
                line_recv(s, k, i).wait_recv()
        for k in range(NY):
            e = s * NY + k
            for way in range(2):
                ynear[way, e] = ol[e, quarter((y + (3, 1)[way]) % NY), :]
                lo = pl.multiple_of(FIRST_B + QUARTER * ((y + 2) % NY) + way * HALF_B, 16)
                yopp[way, e] = ol[e, pl.ds(lo, HALF_B), :]

    def z_copy(way, t):
        return rcopy(
            zst.at[way, t % KEEP], zland.at[way, t], zsend.at[way, t % KEEP], zrecv.at[way, t % KEEP], zn[way]
        )

    def n_copy(way, t):
        return rcopy(yst.at[t], ynear.at[way, OWN + t], nsend.at[way, t % KEEP], nrecv.at[way, t % KEEP_Y], yn[way])

    def p_copy(way, t, direct=False):
        half = pl.ds(way * HALF_B, HALF_B)
        src = yst.at[t, half] if direct else ynear.at[way, OWN + t, half]
        to = ypeer[2] if direct else yn[way]
        recv = precv.at[way, KEEP_Y + t - DIRECT if direct else t % KEEP_Y]
        return rcopy(src, yopp.at[way, OWN + t], psend.at[way, t % KEEP], recv, to)

    def o_take(t):
        for way in range(2):
            p_copy(way, t).wait_recv()

    def entry(*at):
        return jnp.clip(table_s[at], 0, OWN + STEPS - 1)

    def z_send(t, again):
        for way in range(2):
            if again:
                z_copy(way, t - KEEP).wait_send()
            zst[way, t % KEEP] = pool[way, entry(way, z, t)]
            z_copy(way, t).start()

    def z_take(t):
        for way in range(2):
            z_copy(way, t).wait_recv()
            pool[way, OWN + t] = zland[way, t]

    def y_send(t, again):
        for way in range(2):
            yst[t, way * HALF_B : way * HALF_B + HALF_B, :] = zland[way, t, HALF_A:, :]
        for way in range(2):
            if again:
                n_copy(way, t - KEEP).wait_send()
            n_copy(way, t).start()

    def y_take(t, again, direct):
        for way in range(2):
            if not direct:
                n_copy(way, t).wait_recv()
            if again:
                p_copy(way, t - KEEP, direct).wait_send()
            p_copy(way, t, direct).start()

    marks = {0, LAG, LAG + LAG_Y, KEEP, KEEP + LAG, KEEP + LAG + LAG_Y, STEPS, STEPS + LAG, DIRECT + LAG, DIRECT + LAG + LAG_Y, LAG + LAG_Y + LAG_O}

    def steps(a, b):
        cuts = [a] + sorted(k for k in marks if a < k < b) + [b]
        for lo, hi in zip(cuts[:-1], cuts[1:]):
            def body(t, _, lo=lo):
                if LAG <= lo < STEPS + LAG:
                    z_take(t - LAG)
                if lo < STEPS:
                    z_send(t, lo >= KEEP)
                if LAG <= lo < STEPS + LAG:
                    y_send(t - LAG, lo - LAG >= KEEP)
                if LAG + LAG_Y <= lo < DIRECT + LAG + LAG_Y:
                    y_take(t - LAG - LAG_Y, lo - LAG - LAG_Y >= KEEP, False)
                if DIRECT + LAG <= lo < STEPS + LAG:
                    y_take(t - LAG, True, True)
                if LAG + LAG_Y + LAG_O <= lo < STEPS + LAG:
                    o_take(t - LAG - LAG_Y - LAG_O)
                return 0

            lax.fori_loop(lo, hi, body, 0)

    def r_copy(k):
        return rcopy(tile.at[0], rk.at[k], rsend.at[k - 1], rrecv.at[k - 1], rpeer[k])

    def sy_copy(k):
        return rcopy(tile.at[1], ry.at[y], sysend.at[k - 1], syrecv.at[k - 1], ypeer[k])

    def sz_copy(k):
        return rcopy(ry, rz.at[z], szsend.at[k - 1], szrecv.at[k - 1], zpeer[k])

    sub = lax.broadcasted_iota(I32, (8, 128), 0)

    def scale_first():
        own = jnp.zeros((8, 128), F32)
        for i in range(4):
            whole = jnp.sum(jnp.sum(part[i], axis=0, keepdims=True), axis=1, keepdims=True)
            own = jnp.where(sub == i, jnp.broadcast_to(whole, (8, 128)), own)
        tile[0] = own
        rk[0] = own
        for k in range(1, 8):
            r_copy(k).start()

    def scale_second():
        for k in range(1, 8):
            r_copy(k).wait_recv()
        total = rk[0]
        for k in range(1, 8):
            total = total + rk[k]
        out = jnp.zeros((8, 128), F32)
        for s in range(2):
            value = jnp.sqrt(total[2 * s : 2 * s + 1]) / jnp.sqrt(total[2 * s + 1 : 2 * s + 2] + 1e-6)
            out = jnp.where(sub == s, jnp.broadcast_to(value, (8, 128)), out)
        tile[1] = out
        ry[pl.ds(y, 1)] = out[None]
        for k in range(1, 4):
            sy_copy(k).start()

    def sy_recv(k):
        frm = (y + NY - k) % NY
        return rcopy(tile.at[1], ry.at[frm], sysend.at[k - 1], syrecv.at[k - 1], ypeer[k])

    def sz_recv(k):
        frm = (z + NZ - k) % NZ
        return rcopy(ry, rz.at[frm], szsend.at[k - 1], szrecv.at[k - 1], zpeer[k])

    def scale_third():
        for k in range(1, 4):
            sy_recv(k).wait_recv()
        rz[pl.ds(z, 1)] = ry[...][None]
        for k in range(1, 8):
            sz_copy(k).start()

    def put(i, src, dst):
        copy = pltpu.make_async_copy(src, dst, outsem.at[i])
        copy.start()
        puts.append(copy)

    puts = []
    x_own(0)
    loads = [
        pltpu.make_async_copy(src, dst, insem.at[4 + i])
        for i, (src, dst) in enumerate(
            [(grads_h, grads), (left_root_h, left_root), (second_h, second), (left_h, left), (right_h, right)]
        )
    ]
    for k in loads:
        k.start()
    tables, finds, held = schedule(owner, z, y)
    for way in range(2):
        table_v[way] = tables[way]
    finds_out[...] = finds
    table_v[2] = finds
    to_smem = pltpu.make_async_copy(table_v, table_s, lsem.at[0])
    to_smem.start()
    x_forward(0)
    x_own(1)
    for k in loads:
        k.wait()
    put(0, finds_out, finds_o)
    graft(0, held > 0)
    graft(1, held > 1)
    put(1, second_new, second_o)
    x_rest(0)
    x_forward(1)
    x_own(2)
    x_held(0)
    x_done(0)
    mix(0)
    x_held(1)
    precondition(0, 0)
    line_send(0, (0,))
    x_rest(1)
    x_forward(2)
    x_own(3)
    x_done(1)
    for j in (3, 1, 2):
        precondition(0, j)
    line_send(0, (1, 2))
    factors(0, held > 0)
    to_smem.wait()
    line_pool(0)
    steps(0, 1)
    line_send(0, (3, 4, 5))
    x_rest(2)
    x_forward(3)
    steps(1, 2)
    x_held(2)
    x_done(2)
    mix(1)
    x_held(3)
    precondition(1, 0)
    line_send(1, (0,))
    steps(2, 4)
    x_rest(3)
    steps(4, 6)
    x_done(3)
    for j in (3, 1, 2):
        precondition(1, j)
    line_send(1, (1, 2))
    scale_first()
    steps(6, SECOND)
    line_pool(1)
    steps(SECOND, SECOND + 3)
    line_send(1, (3, 4, 5))
    scale_second()
    factors(1, held > 1)
    put(2, left_new, left_o)
    put(3, right_new, right_o)
    steps(SECOND + 3, SECOND + 8)
    scale_third()
    steps(SECOND + 8, SECOND + 18)
    for s in range(2):
        line_rest(s)
    for k in range(1, 8):
        sz_recv(k).wait_recv()
    put(4, rz, sout)
    steps(SECOND + 18, STEPS + LAG)
    for t in range(DIRECT, STEPS):
        for way in range(2):
            n_copy(way, t).wait_recv()
    for t in range(STEPS - LAG_Y - LAG_O, STEPS):
        for way in range(2):
            p_copy(way, t, t >= DIRECT).wait_recv()

    def back(b):
        return pltpu.make_async_copy(rows_out.at[b % 16], blocks_o.at[b], blocksem.at[b % 16])

    def assemble(b, again):
        plus, minus = entry(2, 0, b), entry(2, 1, b)
        if again:
            back(b - 16).wait()
        keep = b % 16
        rows_out[keep, :HALF_A] = pool[0, plus, :HALF_A]
        rows_out[keep, HALF_A:FIRST_B] = pool[1, minus, :HALF_A]

        def fill(q, first, last):
            lo = pl.multiple_of(FIRST_B + QUARTER * (q % NY), 16)
            rows_out[keep, pl.ds(lo, HALF_B)] = first
            rows_out[keep, pl.ds(pl.multiple_of(lo + HALF_B, 16), HALF_B)] = last

        fill(y, pool[0, plus, HALF_A:], pool[1, minus, HALF_A:])
        fill(y + 3, ynear[0, plus, :HALF_B], ynear[0, minus, HALF_B:])
        fill(y + 1, ynear[1, plus, :HALF_B], ynear[1, minus, HALF_B:])
        fill(y + 2, yopp[0, plus], yopp[1, minus])
        back(b).start()
        return 0

    lax.fori_loop(0, 16, lambda b, _: assemble(b, False), 0)
    lax.fori_loop(16, 32, lambda b, _: assemble(b, True), 0)
    for w in range(4):
        x_drain(w)
    for s in range(2):
        for k in range(1, 4):
            for i in range(6):
                line_copy(s, k, i).wait_send()
    for t in range(STEPS - KEEP, STEPS):
        for way in range(2):
            z_copy(way, t).wait_send()
            n_copy(way, t).wait_send()
            p_copy(way, t).wait_send()
    for k in range(1, 8):
        r_copy(k).wait_send()
        sz_copy(k).wait_send()
    for k in range(1, 4):
        sy_copy(k).wait_send()
    for p in puts:
        p.wait()
    for b in range(16, 32):
        back(b).wait()


def scale_kernel(
    finds, blocks, scales, left, right, second, out, left_new, right_new, second_new,
    flat, sv, rows_out, held, insem, blocksem, outsem,
):
    _, _, x, _ = me()
    first = pltpu.make_async_copy(scales, sv, insem.at[3])
    first.start()

    def fetch(b):
        return pltpu.make_async_copy(blocks.at[b], flat.at[b], blocksem.at[b])

    def begin(b, _):
        fetch(b).start()
        return 0

    lax.fori_loop(0, 8, begin, 0)
    through = [
        pltpu.make_async_copy(ref, held.at[i], insem.at[i]) for i, ref in enumerate((left, right, second))
    ]
    for k in through:
        k.start()
    lax.fori_loop(8, 32, begin, 0)
    first.wait()

    def back(b):
        return pltpu.make_async_copy(rows_out.at[b % 8], out.at[b], outsem.at[b % 8])

    def one(b, again):
        owner = jnp.clip(finds[2, b], 0, NY * NZ - 1)
        scale = sv[owner // NY, owner % NY, pl.ds(jnp.clip(finds[3, b], 0, 1), 1), :]
        fetch(b).wait()
        if again:
            back(b - 8).wait()
        for i, j in enumerate(PLACE):
            for half in range(2):
                row = (2 * i + half) * 128
                col = pl.multiple_of((x + j) % NX * 256 + half * 128, 128)
                part = flat[b, row : row + 128, :].astype(F32) * scale
                rows_out[b % 8, :, pl.ds(col, 128)] = part.astype(BF)
        back(b).start()
        return 0

    lax.fori_loop(0, 8, lambda b, _: one(b, False), 0)
    for i, ref in enumerate((left_new, right_new, second_new)):
        through[i].wait()
        through[i] = pltpu.make_async_copy(held.at[i], ref, insem.at[i])
        through[i].start()
    lax.fori_loop(8, 32, lambda b, _: one(b, True), 0)
    for b in range(24, 32):
        back(b).wait()
    for k in through:
        k.wait()


def on_device(grads, left, right, left_root, right_root, second, owner):
    smem, hbm = pl.BlockSpec(memory_space=pltpu.SMEM), pl.BlockSpec(memory_space=pl.ANY)
    shape = jax.ShapeDtypeStruct
    b_shape = (SLOTS_DEV, ROWS, WIDTH)
    block = shape(b_shape, BF)
    s_shape = (NZ, NY, 8, 128)
    stacked = (32, WIDTH, 128)
    entries = OWN + STEPS
    dma = pltpu.SemaphoreType.DMA
    left_new, right_new, second_new, blocks, scales, finds = pl.pallas_call(
        main_kernel,
        out_shape=(
            block, block, block, shape(stacked, BF), shape(s_shape, F32), shape((8, 128), I32),
        ),
        in_specs=[hbm] * 6 + [smem],
        out_specs=(hbm,) * 6,
        scratch_shapes=[pltpu.VMEM(b_shape, BF)] * 8
        + [
            pltpu.VMEM((8, 128), I32),
            pltpu.VMEM((4, WIDTH, WIDTH), BF),
            pltpu.VMEM((ROWS, WIDTH), BF),
            pltpu.VMEM((SLOTS_DEV, WIDTH, 128), BF),
            pltpu.VMEM((OWN, WIDTH, 128), BF),
            pltpu.VMEM((2, STEPS, CHUNK, 128), BF),
            pltpu.VMEM((2, entries, CHUNK, 128), BF),
            pltpu.VMEM((2, KEEP, CHUNK, 128), BF),
            pltpu.VMEM((STEPS, QUARTER, 128), BF),
            pltpu.VMEM((2, entries, QUARTER, 128), BF),
            pltpu.VMEM((2, entries, HALF_B, 128), BF),
            pltpu.VMEM((16, WIDTH, 128), BF),
            pltpu.VMEM((3, 8, 128), I32),
            pltpu.SMEM((3, 8, 128), I32),
            pltpu.VMEM((4, 8, 128), F32),
            pltpu.VMEM((8, 8, 128), F32),
            pltpu.VMEM((NY, 8, 128), F32),
            pltpu.VMEM(s_shape, F32),
            pltpu.VMEM((2, 8, 128), F32),
            dma((4, 10)), dma((4, 10)),
            dma((2, 3, 6)), dma((2, 3, 6)),
            dma((2, KEEP)), dma((2, KEEP)),
            dma((2, KEEP)), dma((2, KEEP_Y)),
            dma((2, KEEP)), dma((2, KEEP_Y + STEPS - DIRECT)),
            dma((7,)), dma((7,)), dma((3,)), dma((3,)), dma((7,)), dma((7,)),
            dma((1,)), dma((9,)), dma((5,)), dma((16,)),
        ],
        compiler_params=pltpu.CompilerParams(
            collective_id=1, has_side_effects=True, vmem_limit_bytes=60 << 20
        ),
        name="shampoo",
    )(grads, left, right, left_root, right_root, second, owner)
    directions, left_new, right_new, second_new = pl.pallas_call(
        scale_kernel,
        out_shape=(shape((32, ROWS, WIDTH), BF), block, block, block),
        in_specs=[smem] + [hbm] * 5,
        out_specs=(hbm,) * 4,
        scratch_shapes=[
            pltpu.VMEM(stacked, BF),
            pltpu.VMEM(s_shape, F32),
            pltpu.VMEM((8, ROWS, WIDTH), BF),
            pltpu.VMEM((3, *b_shape), BF),
            dma((4,)), dma((32,)), dma((8,)),
        ],
        compiler_params=pltpu.CompilerParams(vmem_limit_bytes=60 << 20),
        name="spread",
    )(finds, blocks, scales, left_new, right_new, second_new)
    return (left_new, right_new, second_new, directions)


def solution(mesh):
    block = P("rep", "rack", None)
    return jax.shard_map(
        on_device,
        mesh=mesh,
        in_specs=(block,) * 6 + (P(),),
        out_specs=(block, block, block, P(None, "rack", None)),
        check_vma=False,
    )
```

```python
import functools

import jax
import jax.numpy as jnp
from jax import lax
from jax.experimental import pallas as pl
from jax.experimental.pallas import tpu as pltpu
from jax.sharding import PartitionSpec as P

MESH = pl.DeviceIdType.MESH
BF, F32, I32 = jnp.bfloat16, jnp.float32, jnp.int32

NX, NY, NZ = 4, 4, 8
ROWS, WIDTH, SLOTS_DEV = 128, 1024, 2
PLACE = (0, 3, 1, 2)
HALF_A = 192
QUARTER = 160
HALF_B = QUARTER // 2
FIRST_B = 2 * HALF_A
CHUNK = HALF_A + HALF_B
OWN = SLOTS_DEV * NY
LAG = 3
LAG_Y = 3
SECOND = 10
VARIANTS = (36, 38, 44)
LAST = 4
LAG_O = 3
KEEP_Y = 16
KEEP = 8
ORDER = (
    (0, 0), (0, 1), (0, 2), (1, 0), (0, 3), (1, 1), (0, 4), (1, 2), (0, 5), (1, 3), (0, 6), (1, 4), (1, 5), (1, 6),
)


def me():
    rep, rack = lax.axis_index("rep"), lax.axis_index("rack")
    return rep // NY, rep % NY, rack // 2, rack % 2


def dev(z, y, x, c):
    return (z * NY + y, x * 2 + c)


def rcopy(src, dst, send, recv, to):
    return pltpu.make_async_remote_copy(
        src_ref=src, dst_ref=dst, send_sem=send, recv_sem=recv, device_id=to, device_id_type=MESH
    )


def schedule(owner, z, y):
    row = lax.broadcasted_iota(I32, (8, 128), 0)
    lane = lax.broadcasted_iota(I32, (8, 128), 1)
    own = jnp.full((8, 128), -1, I32)
    owner_col = jnp.zeros((32, 128), I32)
    sub = lax.broadcasted_iota(I32, (32, 128), 0)
    for b in range(32):
        own = jnp.where(lane == b, owner[b], own)
        owner_col = jnp.where(sub == b, owner[b], owner_col)
    owner_row = own[:1]
    cnt = [
        jnp.broadcast_to(
            jnp.sum((own == row * NY + k).astype(I32), axis=1, keepdims=True), (8, 128)
        )
        for k in range(NY)
    ]
    used = [[(c > p).astype(I32) for c in cnt] for p in range(SLOTS_DEV)]
    size = [u[0] + u[1] + u[2] + u[3] for u in used]
    before = [[sum(u[:k], jnp.zeros((8, 128), I32)) for k in range(NY)] for u in used]
    start = []
    tables = []
    ends = []
    for turn in (1, -1):
        st = {}
        end = jnp.zeros((8, 128), I32)
        table = jnp.zeros((8, 128), I32)
        for p, d in ORDER:
            at = end
            if p == 1 and d == 0:
                at = jnp.maximum(at, SECOND)
            if d > 0:
                came = pltpu.roll(st[p, d - 1], turn % 8, 0)
                at = jnp.maximum(at, came + LAG)
            st[p, d] = at
            count = size[p] if d == 0 else pltpu.roll(size[p], (turn * d) % 8, 0)
            end = at + count
            spot = lane - at
            if d == 0:
                entry = jnp.zeros((8, 128), I32)
                for k in range(NY):
                    hit = (used[p][k] == 1) & (before[p][k] == spot)
                    entry = entry + jnp.where(hit, p * NY + k, 0)
            else:
                entry = OWN + came + spot
            table = jnp.where((lane >= at) & (lane < end), entry, table)
        start.append(st)
        ends.append(end)
        tables.append(table)
    earlier = (owner_col == owner_row) & (
        lax.broadcasted_iota(I32, (32, 128), 0) < lax.broadcasted_iota(I32, (32, 128), 1)
    )
    slot = jnp.broadcast_to(jnp.sum(earlier.astype(I32), axis=0, keepdims=True), (8, 128))
    zb, yb = own >> 2, own & 3
    rank = jnp.zeros((8, 128), I32)
    for k in range(NY):
        line = jnp.sum((owner_col == (owner_row >> 2) * NY + k).astype(I32), axis=0, keepdims=True)
        line = jnp.broadcast_to(line, (8, 128))
        rank = rank + ((line > slot) & (yb > k)).astype(I32)
    here = zb == z
    found = []
    for way, turn in enumerate((1, -1)):
        hops = (turn * (z - zb)) & 7
        came_at = jnp.zeros((8, 128), I32)
        sender = (z - turn) & 7
        for p in range(SLOTS_DEV):
            for d in range(7):
                st = jnp.sum(jnp.where(row == sender, start[way][p, d], 0), axis=0, keepdims=True)
                came_at = jnp.where((hops == d + 1) & (slot == p), st + rank, came_at)
        found.append(jnp.where(here, slot * NY + yb, OWN + came_at))
    finds = jnp.where(row == 0, found[0], 0)
    finds = jnp.where(row == 1, found[1], finds)
    finds = jnp.where(row == 2, own, finds)
    finds = jnp.where(row == 3, slot, finds)
    held = jnp.sum((own == z * NY + y).astype(I32), axis=1, keepdims=True)
    finds = jnp.where(row == 4, held, finds)
    ends = jnp.maximum(ends[0], ends[1])
    return tables, finds, jnp.max(ends)


def plan_kernel(owner, tables_o, finds_o, which_o):
    z, y, _, _ = me()
    tables, finds, ends = schedule(owner, z, y)
    for way in range(2):
        tables_o[way] = tables[way]
    tables_o[2] = finds
    finds_o[...] = finds
    which = jnp.int32(0)
    for some in VARIANTS[:-1]:
        which = which + (ends > some).astype(I32)
    which_o[0] = which


def main_kernel(
    STEPS, grads_h, left_h, right_h, left_root_h, right_root_h, second_h, tables_h,
    left_o, right_o, second_o, blocks_o, sout,
    grads, left, right, left_root, second, left_new, right_new, second_new, xb, mixed, stack, ol, zland, pool, zst, yst, ynear, yopp, rows_out,
    table_s, part, rk, ry, rz, tile,
    xsend, xrecv, osend, orecv, zsend, zrecv, nsend, nrecv, psend, precv,
    rsend, rrecv, sysend, syrecv, szsend, szrecv, lsem, insem, outsem, blocksem,
):
    DIRECT = STEPS - LAST
    z, y, x, c = me()
    rack = x * 2 + c
    xp, xm = dev(z, y, (x + 1) % NX, c), dev(z, y, (x + NX - 1) % NX, c)
    sibling = dev(z, y, x, 1 - c)
    ypeer = [None] + [dev(z, (y + k) % NY, x, c) for k in range(1, NY)]
    zpeer = [None] + [dev((z + k) % NZ, y, x, c) for k in range(1, NZ)]
    rpeer = [None] + [(z * NY + y, (rack + k) % 8) for k in range(1, 8)]
    yn = (ypeer[1], ypeer[3])
    zn = (zpeer[1], zpeer[7])

    barrier = pltpu.get_barrier_semaphore()
    peers = ypeer[1:] + zpeer[1:] + rpeer[1:]
    for p in peers:
        pl.semaphore_signal(barrier, inc=1, device_id=p, device_id_type=MESH)
    pl.semaphore_wait(barrier, len(peers))

    after, two, prior = (x + 1) % NX, (x + 2) % NX, (x + 3) % NX

    def source(w):
        return (grads_h, right_root_h)[w % 2].at[w // 2]

    def brow(xx, cc, lo=0, n=ROWS):
        return pl.ds(pl.multiple_of((xx * 2 + cc) * ROWS + lo, 64), n)

    def bcol(xx):
        return pl.ds(pl.multiple_of(xx * 256, 256), 256)

    def x_copy(w, k):
        if w % 2 == 0:
            lo = (0, 64, 64, 0, 0, 64)[k]
            to = (xp, xp, xm, xm, xp, xm)[k]
            if k < 4:
                src, dst = source(w).at[lo : lo + 64], xb.at[w, brow(x, c, lo, 64)]
            else:
                src = dst = xb.at[w, brow(prior if k == 4 else after, c, lo, 64)]
        else:
            to = (xp, xp, xp, xm, xm, xm)[k]
            col = bcol((x, prior, two, x, after, after)[k])
            if k < 5:
                src, dst = source(w).at[:, col], xb.at[w, brow(x, c), col]
            else:
                src = dst = xb.at[w, brow(after, c), col]
        return rcopy(src, dst, xsend.at[w, k], xrecv.at[w, k], to)

    def core_copy(w, i):
        rows = brow((x, prior, after, two)[i], c)
        src = source(w) if i == 0 else xb.at[w, rows]
        return rcopy(src, xb.at[w, rows], xsend.at[w, 6 + i], xrecv.at[w, 6 + i], sibling)

    def own_copy(w):
        return pltpu.make_async_copy(source(w), xb.at[w, brow(x, c)], insem.at[w])

    def x_own(w):
        for k in ((0, 2, 1, 3), (3, 0, 4, 1, 2))[w % 2]:
            x_copy(w, k).start()
        core_copy(w, 0).start()
        own_copy(w).start()

    def x_forward(w):
        for k, on in (((0, 4), (2, 5)), ((3, 5),))[w % 2]:
            x_copy(w, k).wait_recv()
            x_copy(w, on).start()

    def x_rest(w):
        for i, ks in enumerate((((1,), (3,), (4, 5)), ((0, 1, 2), (4,), (5,)))[w % 2]):
            for k in ks:
                x_copy(w, k).wait_recv()
            core_copy(w, 1 + i).start()

    def x_held(w):
        own_copy(w).wait()
        core_copy(w, 0).wait_recv()

    def x_done(w):
        for i in range(1, 4):
            core_copy(w, i).wait_recv()

    def x_drain(w):
        for k in range(6):
            x_copy(w, k).wait_send()
        for i in range(4):
            core_copy(w, i).wait_send()

    def mix(s):
        for m in range(4):
            cols = slice(m * 256, m * 256 + 256)
            mixed[:, cols] = jnp.dot(left_root[s], xb[2 * s, :, cols], preferred_element_type=F32).astype(BF)

    def precondition(s, j):
        w = 2 * s + 1
        at = PLACE.index(j) * 256
        got = jnp.zeros((ROWS, 256), F32)
        for i in range(4):
            lhs = mixed[:, bcol((x + i) % NX)]
            here = i == 0 or (i, j) in ((3, 1), (3, 2), (3, 3), (1, 1), (1, 2), (2, 2))
            r, k = (i, j) if here else (j, i)
            block = xb[w, bcol((x + r) % NX), bcol((x + k) % NX)]
            got += lax.dot_general(
                lhs, block, (((1,), (0 if here else 1,)), ((), ())), preferred_element_type=F32
            )
        got_b = got.astype(BF)
        stack[s, at : at + 128, :] = got_b[:, :128]
        stack[s, at + 128 : at + 256, :] = got_b[:, 128:]
        sq = got * got
        sq = jnp.sum((sq[:, :128] + sq[:, 128:]).reshape(16, 8, 128), axis=0)
        part[2 * s + 1] = sq if j == 0 else part[2 * s + 1] + sq

    def factors(s, keep):
        for m in range(4):
            cols = slice(m * 256, m * 256 + 256)
            outer = lax.dot_general(
                grads[s], xb[2 * s, cols, :], (((1,), (1,)), ((), ())), preferred_element_type=F32
            )
            old = left[s, :, cols].astype(F32)
            left_new[s, :, cols] = jnp.where(keep, 0.95 * old + 0.05 * outer, old).astype(BF)
        mine = xb[2 * s, :, pl.ds(pl.multiple_of(rack * 128, 128), 128)]
        for m in range(4):
            cols = slice(m * 256, m * 256 + 256)
            inner = lax.dot_general(
                mine, xb[2 * s, :, cols], (((0,), (0,)), ((), ())), preferred_element_type=F32
            )
            old = right[s, :, cols].astype(F32)
            new = 0.95 * old + 0.05 * inner
            right_new[s, :, cols] = jnp.where(keep, new, old).astype(BF)

    def graft(s, keep):
        def tile_rows(i, total):
            rows = pl.ds(pl.multiple_of(i * 16, 16), 16)
            g = grads[s, rows, :].astype(F32)
            old = second[s, rows, :].astype(F32)
            moment = 0.95 * old + 0.05 * g * g
            second_new[s, rows, :] = jnp.where(keep, moment, old).astype(BF)
            adam = g / (jnp.sqrt(moment) + 1e-8)
            return total + adam * adam

        total = lax.fori_loop(0, 8, tile_rows, jnp.zeros((16, WIDTH), F32))
        total = jnp.sum(total.reshape(2, 8, WIDTH), axis=0)
        acc = total[:, :128]
        for k in range(1, 8):
            acc = acc + total[:, k * 128 : k * 128 + 128]
        part[2 * s] = acc

    def quarter(k):
        return pl.ds(pl.multiple_of(FIRST_B + QUARTER * k, 16), QUARTER)

    def line_part(s, k, i, sender, receiver):
        if i < 2:
            rows = pl.ds(0, 256) if i == 0 else pl.ds(256, FIRST_B - 256)
        else:
            rows = quarter((receiver + i - 2) % NY)
        return rcopy(
            stack.at[s, rows], ol.at[s * NY + sender, rows], osend.at[s, k - 1, i], orecv.at[s, k - 1, i], ypeer[k]
        )

    def line_copy(s, k, i):
        return line_part(s, k, i, y, (y + k) % NY)

    def line_recv(s, k, i):
        return line_part(s, k, i, (y + NY - k) % NY, y)

    def line_send(s, parts):
        for i in parts:
            for k in (1, 3, 2):
                line_copy(s, k, i).start()

    def line_pool(s):
        ol[pl.ds(s * NY + y, 1)] = stack[s][None]
        for i in (0, 1, 2):
            for k in (1, 3, 2):
                line_recv(s, k, i).wait_recv()
        for k in range(NY):
            e = s * NY + k
            for way in range(2):
                pool[way, e, :HALF_A] = ol[e, way * HALF_A : way * HALF_A + HALF_A, :]
                lo = pl.multiple_of(FIRST_B + QUARTER * y + way * HALF_B, 16)
                pool[way, e, HALF_A:] = ol[e, pl.ds(lo, HALF_B), :]

    def line_rest(s):
        for i in (3, 4, 5):
            for k in (1, 3, 2):
                line_recv(s, k, i).wait_recv()
        for k in range(NY):
            e = s * NY + k
            for way in range(2):
                ynear[way, e] = ol[e, quarter((y + (3, 1)[way]) % NY), :]
                lo = pl.multiple_of(FIRST_B + QUARTER * ((y + 2) % NY) + way * HALF_B, 16)
                yopp[way, e] = ol[e, pl.ds(lo, HALF_B), :]

    def z_copy(way, t):
        return rcopy(
            zst.at[way, t % KEEP], zland.at[way, t], zsend.at[way, t % KEEP], zrecv.at[way, t % KEEP], zn[way]
        )

    def n_copy(way, t):
        return rcopy(yst.at[t], ynear.at[way, OWN + t], nsend.at[way, t % KEEP], nrecv.at[way, t % KEEP_Y], yn[way])

    def p_copy(way, t, direct=False):
        half = pl.ds(way * HALF_B, HALF_B)
        src = yst.at[t, half] if direct else ynear.at[way, OWN + t, half]
        to = ypeer[2] if direct else yn[way]
        recv = precv.at[way, KEEP_Y + t - DIRECT if direct else t % KEEP_Y]
        return rcopy(src, yopp.at[way, OWN + t], psend.at[way, t % KEEP], recv, to)

    def o_take(t):
        for way in range(2):
            p_copy(way, t).wait_recv()

    def entry(*at):
        return jnp.clip(table_s[at], 0, OWN + STEPS - 1)

    def z_send(t, again):
        for way in range(2):
            if again:
                z_copy(way, t - KEEP).wait_send()
            zst[way, t % KEEP] = pool[way, entry(way, z, t)]
            z_copy(way, t).start()

    def z_take(t):
        for way in range(2):
            z_copy(way, t).wait_recv()
            pool[way, OWN + t] = zland[way, t]

    def y_send(t, again):
        for way in range(2):
            yst[t, way * HALF_B : way * HALF_B + HALF_B, :] = zland[way, t, HALF_A:, :]
        for way in range(2):
            if again:
                n_copy(way, t - KEEP).wait_send()
            n_copy(way, t).start()

    def y_take(t, again, direct):
        for way in range(2):
            if not direct:
                n_copy(way, t).wait_recv()
            if again:
                p_copy(way, t - KEEP, direct).wait_send()
            p_copy(way, t, direct).start()

    marks = {0, LAG, LAG + LAG_Y, KEEP, KEEP + LAG, KEEP + LAG + LAG_Y, STEPS, STEPS + LAG, DIRECT + LAG, DIRECT + LAG + LAG_Y, LAG + LAG_Y + LAG_O}

    def steps(a, b):
        cuts = [a] + sorted(k for k in marks if a < k < b) + [b]
        for lo, hi in zip(cuts[:-1], cuts[1:]):
            def body(t, _, lo=lo):
                if LAG <= lo < STEPS + LAG:
                    z_take(t - LAG)
                if lo < STEPS:
                    z_send(t, lo >= KEEP)
                if LAG <= lo < STEPS + LAG:
                    y_send(t - LAG, lo - LAG >= KEEP)
                if LAG + LAG_Y <= lo < DIRECT + LAG + LAG_Y:
                    y_take(t - LAG - LAG_Y, lo - LAG - LAG_Y >= KEEP, False)
                if DIRECT + LAG <= lo < STEPS + LAG:
                    y_take(t - LAG, True, True)
                if LAG + LAG_Y + LAG_O <= lo < STEPS + LAG:
                    o_take(t - LAG - LAG_Y - LAG_O)
                return 0

            lax.fori_loop(lo, hi, body, 0)

    def r_copy(k):
        return rcopy(tile.at[0], rk.at[k], rsend.at[k - 1], rrecv.at[k - 1], rpeer[k])

    def sy_copy(k):
        return rcopy(tile.at[1], ry.at[y], sysend.at[k - 1], syrecv.at[k - 1], ypeer[k])

    def sz_copy(k):
        return rcopy(ry, rz.at[z], szsend.at[k - 1], szrecv.at[k - 1], zpeer[k])

    sub = lax.broadcasted_iota(I32, (8, 128), 0)

    def scale_first():
        own = jnp.zeros((8, 128), F32)
        for i in range(4):
            whole = jnp.sum(jnp.sum(part[i], axis=0, keepdims=True), axis=1, keepdims=True)
            own = jnp.where(sub == i, jnp.broadcast_to(whole, (8, 128)), own)
        tile[0] = own
        rk[0] = own
        for k in range(1, 8):
            r_copy(k).start()

    def scale_second():
        for k in range(1, 8):
            r_copy(k).wait_recv()
        total = rk[0]
        for k in range(1, 8):
            total = total + rk[k]
        out = jnp.zeros((8, 128), F32)
        for s in range(2):
            value = jnp.sqrt(total[2 * s : 2 * s + 1]) / jnp.sqrt(total[2 * s + 1 : 2 * s + 2] + 1e-6)
            out = jnp.where(sub == s, jnp.broadcast_to(value, (8, 128)), out)
        tile[1] = out
        ry[pl.ds(y, 1)] = out[None]
        for k in range(1, 4):
            sy_copy(k).start()

    def sy_recv(k):
        frm = (y + NY - k) % NY
        return rcopy(tile.at[1], ry.at[frm], sysend.at[k - 1], syrecv.at[k - 1], ypeer[k])

    def sz_recv(k):
        frm = (z + NZ - k) % NZ
        return rcopy(ry, rz.at[frm], szsend.at[k - 1], szrecv.at[k - 1], zpeer[k])

    def scale_third():
        for k in range(1, 4):
            sy_recv(k).wait_recv()
        rz[pl.ds(z, 1)] = ry[...][None]
        for k in range(1, 8):
            sz_copy(k).start()

    def put(i, src, dst):
        copy = pltpu.make_async_copy(src, dst, outsem.at[i])
        copy.start()
        puts.append(copy)

    puts = []
    x_own(0)
    loads = [
        pltpu.make_async_copy(src, dst, insem.at[4 + i])
        for i, (src, dst) in enumerate(
            [(grads_h, grads), (left_root_h, left_root), (second_h, second), (left_h, left), (right_h, right)]
        )
    ]
    for k in loads:
        k.start()
    to_smem = pltpu.make_async_copy(tables_h, table_s, lsem.at[0])
    to_smem.start()
    x_forward(0)
    x_own(1)
    for k in loads:
        k.wait()
    to_smem.wait()
    held = jnp.zeros((1, 1), I32) + table_s[2, 4, 0]
    graft(0, held > 0)
    graft(1, held > 1)
    put(0, second_new, second_o)
    x_rest(0)
    x_forward(1)
    x_own(2)
    x_held(0)
    x_done(0)
    mix(0)
    x_held(1)
    precondition(0, 0)
    line_send(0, (0,))
    x_rest(1)
    x_forward(2)
    x_own(3)
    x_done(1)
    for j in (3, 1, 2):
        precondition(0, j)
    line_send(0, (1, 2))
    factors(0, held > 0)
    line_pool(0)
    steps(0, 1)
    x_rest(2)
    x_forward(3)
    steps(1, 2)
    x_held(2)
    x_done(2)
    mix(1)
    x_held(3)
    precondition(1, 0)
    line_send(1, (0,))
    steps(2, 4)
    x_rest(3)
    steps(4, 6)
    x_done(3)
    for j in (3, 1, 2):
        precondition(1, j)
    line_send(1, (1, 2))
    scale_first()
    steps(6, SECOND)
    line_pool(1)
    steps(SECOND, SECOND + 3)
    scale_second()
    factors(1, held > 1)
    put(2, left_new, left_o)
    put(3, right_new, right_o)
    steps(SECOND + 3, SECOND + 5)
    line_send(0, (3,))
    steps(SECOND + 5, SECOND + 8)
    line_send(0, (4,))
    scale_third()
    steps(SECOND + 8, SECOND + 10)
    line_send(0, (5,))
    steps(SECOND + 10, SECOND + 12)
    line_send(1, (3,))
    steps(SECOND + 12, SECOND + 15)
    line_send(1, (4,))
    steps(SECOND + 15, SECOND + 18)
    line_send(1, (5,))
    steps(SECOND + 18, SECOND + 26)
    for s in range(2):
        line_rest(s)
    for k in range(1, 8):
        sz_recv(k).wait_recv()
    put(1, rz, sout)
    steps(SECOND + 26, STEPS + LAG)
    for t in range(DIRECT, STEPS):
        for way in range(2):
            n_copy(way, t).wait_recv()
    for t in range(STEPS - LAG_Y - LAG_O, STEPS):
        for way in range(2):
            p_copy(way, t, t >= DIRECT).wait_recv()

    def back(b):
        return pltpu.make_async_copy(rows_out.at[b % 16], blocks_o.at[b], blocksem.at[b % 16])

    def assemble(b, again):
        plus, minus = entry(2, 0, b), entry(2, 1, b)
        if again:
            back(b - 16).wait()
        keep = b % 16
        rows_out[keep, :HALF_A] = pool[0, plus, :HALF_A]
        rows_out[keep, HALF_A:FIRST_B] = pool[1, minus, :HALF_A]

        def fill(q, first, last):
            lo = pl.multiple_of(FIRST_B + QUARTER * (q % NY), 16)
            rows_out[keep, pl.ds(lo, HALF_B)] = first
            rows_out[keep, pl.ds(pl.multiple_of(lo + HALF_B, 16), HALF_B)] = last

        fill(y, pool[0, plus, HALF_A:], pool[1, minus, HALF_A:])
        fill(y + 3, ynear[0, plus, :HALF_B], ynear[0, minus, HALF_B:])
        fill(y + 1, ynear[1, plus, :HALF_B], ynear[1, minus, HALF_B:])
        fill(y + 2, yopp[0, plus], yopp[1, minus])
        back(b).start()
        return 0

    lax.fori_loop(0, 16, lambda b, _: assemble(b, False), 0)
    lax.fori_loop(16, 32, lambda b, _: assemble(b, True), 0)
    for w in range(4):
        x_drain(w)
    for s in range(2):
        for k in range(1, 4):
            for i in range(6):
                line_copy(s, k, i).wait_send()
    for t in range(STEPS - KEEP, STEPS):
        for way in range(2):
            z_copy(way, t).wait_send()
            n_copy(way, t).wait_send()
            p_copy(way, t).wait_send()
    for k in range(1, 8):
        r_copy(k).wait_send()
        sz_copy(k).wait_send()
    for k in range(1, 4):
        sy_copy(k).wait_send()
    for p in puts:
        p.wait()
    for b in range(16, 32):
        back(b).wait()


def scale_kernel(
    finds, blocks, scales, left, right, second, out, left_new, right_new, second_new,
    flat, sv, rows_out, held, insem, blocksem, outsem,
):
    _, _, x, _ = me()
    first = pltpu.make_async_copy(scales, sv, insem.at[3])
    first.start()

    def fetch(b):
        return pltpu.make_async_copy(blocks.at[b], flat.at[b], blocksem.at[b])

    def begin(b, _):
        fetch(b).start()
        return 0

    lax.fori_loop(0, 8, begin, 0)
    through = [
        pltpu.make_async_copy(ref, held.at[i], insem.at[i]) for i, ref in enumerate((left, right, second))
    ]
    for k in through:
        k.start()
    lax.fori_loop(8, 32, begin, 0)
    first.wait()

    def back(b):
        return pltpu.make_async_copy(rows_out.at[b % 8], out.at[b], outsem.at[b % 8])

    def one(b, again):
        owner = jnp.clip(finds[2, b], 0, NY * NZ - 1)
        scale = sv[owner // NY, owner % NY, pl.ds(jnp.clip(finds[3, b], 0, 1), 1), :]
        fetch(b).wait()
        if again:
            back(b - 8).wait()
        for i, j in enumerate(PLACE):
            for half in range(2):
                row = (2 * i + half) * 128
                col = pl.multiple_of((x + j) % NX * 256 + half * 128, 128)
                part = flat[b, row : row + 128, :].astype(F32) * scale
                rows_out[b % 8, :, pl.ds(col, 128)] = part.astype(BF)
        back(b).start()
        return 0

    lax.fori_loop(0, 8, lambda b, _: one(b, False), 0)
    for i, ref in enumerate((left_new, right_new, second_new)):
        through[i].wait()
        through[i] = pltpu.make_async_copy(held.at[i], ref, insem.at[i])
        through[i].start()
    lax.fori_loop(8, 32, lambda b, _: one(b, True), 0)
    for b in range(24, 32):
        back(b).wait()
    for k in through:
        k.wait()


def on_device(grads, left, right, left_root, right_root, second, owner):
    smem, hbm = pl.BlockSpec(memory_space=pltpu.SMEM), pl.BlockSpec(memory_space=pl.ANY)
    vmem = pl.BlockSpec(memory_space=pltpu.VMEM)
    shape = jax.ShapeDtypeStruct
    b_shape = (SLOTS_DEV, ROWS, WIDTH)
    block = shape(b_shape, BF)
    tables, finds, which = pl.pallas_call(
        plan_kernel,
        out_shape=(shape((3, 8, 128), I32), shape((8, 128), I32), shape((1,), I32)),
        in_specs=[smem],
        out_specs=(vmem, vmem, smem),
        name="plan",
    )(owner)
    s_shape = (NZ, NY, 8, 128)
    dma = pltpu.SemaphoreType.DMA
    stacked = (32, WIDTH, 128)

    def run(i, *args):
        STEPS = VARIANTS[i]
        entries = OWN + STEPS
        return pl.pallas_call(
            functools.partial(main_kernel, STEPS),
            out_shape=(
                block, block, block, shape(stacked, BF), shape(s_shape, F32),
            ),
            in_specs=[hbm] * 7,
            out_specs=(hbm,) * 5,
            scratch_shapes=[pltpu.VMEM(b_shape, BF)] * 8
            + [
                pltpu.VMEM((4, WIDTH, WIDTH), BF),
                pltpu.VMEM((ROWS, WIDTH), BF),
                pltpu.VMEM((SLOTS_DEV, WIDTH, 128), BF),
                pltpu.VMEM((OWN, WIDTH, 128), BF),
                pltpu.VMEM((2, STEPS, CHUNK, 128), BF),
                pltpu.VMEM((2, entries, CHUNK, 128), BF),
                pltpu.VMEM((2, KEEP, CHUNK, 128), BF),
                pltpu.VMEM((STEPS, QUARTER, 128), BF),
                pltpu.VMEM((2, entries, QUARTER, 128), BF),
                pltpu.VMEM((2, entries, HALF_B, 128), BF),
                pltpu.VMEM((16, WIDTH, 128), BF),
                pltpu.SMEM((3, 8, 128), I32),
                pltpu.VMEM((4, 8, 128), F32),
                pltpu.VMEM((8, 8, 128), F32),
                pltpu.VMEM((NY, 8, 128), F32),
                pltpu.VMEM(s_shape, F32),
                pltpu.VMEM((2, 8, 128), F32),
                dma((4, 10)), dma((4, 10)),
                dma((2, 3, 6)), dma((2, 3, 6)),
                dma((2, KEEP)), dma((2, KEEP)),
                dma((2, KEEP)), dma((2, KEEP_Y)),
                dma((2, KEEP)), dma((2, KEEP_Y + LAST)),
                dma((7,)), dma((7,)), dma((3,)), dma((3,)), dma((7,)), dma((7,)),
                dma((1,)), dma((9,)), dma((4,)), dma((16,)),
            ],
            compiler_params=pltpu.CompilerParams(
                collective_id=1 + i, has_side_effects=True, vmem_limit_bytes=60 << 20
            ),
            name="shampoo",
        )(*args)

    left_new, right_new, second_new, blocks, scales = lax.switch(
        which[0],
        [functools.partial(run, i) for i in range(len(VARIANTS))],
        grads, left, right, left_root, right_root, second, tables,
    )
    directions, left_new, right_new, second_new = pl.pallas_call(
        scale_kernel,
        out_shape=(shape((32, ROWS, WIDTH), BF), block, block, block),
        in_specs=[smem] + [hbm] * 5,
        out_specs=(hbm,) * 4,
        scratch_shapes=[
            pltpu.VMEM(stacked, BF),
            pltpu.VMEM(s_shape, F32),
            pltpu.VMEM((8, ROWS, WIDTH), BF),
            pltpu.VMEM((3, *b_shape), BF),
            dma((4,)), dma((32,)), dma((8,)),
        ],
        compiler_params=pltpu.CompilerParams(vmem_limit_bytes=60 << 20),
        name="spread",
    )(finds, blocks, scales, left_new, right_new, second_new)
    return (left_new, right_new, second_new, directions)


def solution(mesh):
    block = P("rep", "rack", None)
    return jax.shard_map(
        on_device,
        mesh=mesh,
        in_specs=(block,) * 6 + (P(),),
        out_specs=(block, block, block, P(None, "rack", None)),
        check_vma=False,
    )
```

```python
import functools

import jax
import jax.numpy as jnp
from jax import lax
from jax.experimental import pallas as pl
from jax.experimental.pallas import tpu as pltpu
from jax.sharding import PartitionSpec as P

MESH = pl.DeviceIdType.MESH
BF, F32, I32 = jnp.bfloat16, jnp.float32, jnp.int32

NX, NY, NZ = 4, 4, 8
ROWS, WIDTH, SLOTS_DEV = 128, 1024, 2
PLACE = (0, 3, 1, 2)
HALF_A = 192
QUARTER = 160
HALF_B = QUARTER // 2
FIRST_B = 2 * HALF_A
CHUNK = HALF_A + HALF_B
OWN = SLOTS_DEV * NY
LAG = 3
LAG_Y = 3
SECOND = 10
VARIANTS = (36, 38, 44)
LAST = 4
LAG_O = 3
KEEP_Y = 16
KEEP = 8
ORDER = (
    (0, 0), (0, 1), (0, 2), (1, 0), (0, 3), (1, 1), (0, 4), (1, 2), (0, 5), (1, 3), (0, 6), (1, 4), (1, 5), (1, 6),
)


def me():
    rep, rack = lax.axis_index("rep"), lax.axis_index("rack")
    return rep // NY, rep % NY, rack // 2, rack % 2


def dev(z, y, x, c):
    return (z * NY + y, x * 2 + c)


def rcopy(src, dst, send, recv, to):
    return pltpu.make_async_remote_copy(
        src_ref=src, dst_ref=dst, send_sem=send, recv_sem=recv, device_id=to, device_id_type=MESH
    )


def schedule(owner, z, y):
    row = lax.broadcasted_iota(I32, (8, 128), 0)
    lane = lax.broadcasted_iota(I32, (8, 128), 1)
    own = jnp.full((8, 128), -1, I32)
    owner_col = jnp.zeros((32, 128), I32)
    sub = lax.broadcasted_iota(I32, (32, 128), 0)
    for b in range(32):
        own = jnp.where(lane == b, owner[b], own)
        owner_col = jnp.where(sub == b, owner[b], owner_col)
    owner_row = own[:1]
    cnt = [
        jnp.broadcast_to(
            jnp.sum((own == row * NY + k).astype(I32), axis=1, keepdims=True), (8, 128)
        )
        for k in range(NY)
    ]
    used = [[(c > p).astype(I32) for c in cnt] for p in range(SLOTS_DEV)]
    size = [u[0] + u[1] + u[2] + u[3] for u in used]
    before = [[sum(u[:k], jnp.zeros((8, 128), I32)) for k in range(NY)] for u in used]
    start = []
    tables = []
    ends = []
    for turn in (1, -1):
        st = {}
        end = jnp.zeros((8, 128), I32)
        table = jnp.zeros((8, 128), I32)
        for p, d in ORDER:
            at = end
            if p == 1 and d == 0:
                at = jnp.maximum(at, SECOND)
            if d > 0:
                came = pltpu.roll(st[p, d - 1], turn % 8, 0)
                at = jnp.maximum(at, came + LAG)
            st[p, d] = at
            count = size[p] if d == 0 else pltpu.roll(size[p], (turn * d) % 8, 0)
            end = at + count
            spot = lane - at
            if d == 0:
                entry = jnp.zeros((8, 128), I32)
                for k in range(NY):
                    hit = (used[p][k] == 1) & (before[p][k] == spot)
                    entry = entry + jnp.where(hit, p * NY + k, 0)
            else:
                entry = OWN + came + spot
            table = jnp.where((lane >= at) & (lane < end), entry, table)
        start.append(st)
        ends.append(end)
        tables.append(table)
    earlier = (owner_col == owner_row) & (
        lax.broadcasted_iota(I32, (32, 128), 0) < lax.broadcasted_iota(I32, (32, 128), 1)
    )
    slot = jnp.broadcast_to(jnp.sum(earlier.astype(I32), axis=0, keepdims=True), (8, 128))
    zb, yb = own >> 2, own & 3
    rank = jnp.zeros((8, 128), I32)
    for k in range(NY):
        line = jnp.sum((owner_col == (owner_row >> 2) * NY + k).astype(I32), axis=0, keepdims=True)
        line = jnp.broadcast_to(line, (8, 128))
        rank = rank + ((line > slot) & (yb > k)).astype(I32)
    here = zb == z
    found = []
    for way, turn in enumerate((1, -1)):
        hops = (turn * (z - zb)) & 7
        came_at = jnp.zeros((8, 128), I32)
        sender = (z - turn) & 7
        for p in range(SLOTS_DEV):
            for d in range(7):
                st = jnp.sum(jnp.where(row == sender, start[way][p, d], 0), axis=0, keepdims=True)
                came_at = jnp.where((hops == d + 1) & (slot == p), st + rank, came_at)
        found.append(jnp.where(here, slot * NY + yb, OWN + came_at))
    finds = jnp.where(row == 0, found[0], 0)
    finds = jnp.where(row == 1, found[1], finds)
    finds = jnp.where(row == 2, own, finds)
    finds = jnp.where(row == 3, slot, finds)
    held = jnp.sum((own == z * NY + y).astype(I32), axis=1, keepdims=True)
    finds = jnp.where(row == 4, held, finds)
    ends = jnp.maximum(ends[0], ends[1])
    return tables, finds, jnp.max(ends)


def plan_kernel(owner, tables_o, finds_o, which_o):
    z, y, _, _ = me()
    tables, finds, ends = schedule(owner, z, y)
    for way in range(2):
        tables_o[way] = tables[way]
    tables_o[2] = finds
    finds_o[...] = finds
    which = jnp.int32(0)
    for some in VARIANTS[:-1]:
        which = which + (ends > some).astype(I32)
    which_o[0] = which


def main_kernel(
    STEPS, grads_h, left_h, right_h, left_root_h, right_root_h, second_h, tables_h,
    left_o, right_o, second_o, blocks_o, sout,
    grads, left, right, left_root, second, left_new, right_new, second_new, xb, mixed, stack, ol, zland, pool, zst, yst, ynear, yopp, rows_out,
    table_s, part, rk, ry, rz, tile,
    xsend, xrecv, osend, orecv, fsend, frecv, zsend, zrecv, nsend, nrecv, psend, precv,
    rsend, rrecv, sysend, syrecv, szsend, szrecv, lsem, insem, outsem, blocksem,
):
    DIRECT = STEPS - LAST
    z, y, x, c = me()
    rack = x * 2 + c
    xp, xm = dev(z, y, (x + 1) % NX, c), dev(z, y, (x + NX - 1) % NX, c)
    sibling = dev(z, y, x, 1 - c)
    ypeer = [None] + [dev(z, (y + k) % NY, x, c) for k in range(1, NY)]
    zpeer = [None] + [dev((z + k) % NZ, y, x, c) for k in range(1, NZ)]
    rpeer = [None] + [(z * NY + y, (rack + k) % 8) for k in range(1, 8)]
    yn = (ypeer[1], ypeer[3])
    zn = (zpeer[1], zpeer[7])

    barrier = pltpu.get_barrier_semaphore()
    peers = ypeer[1:] + zpeer[1:] + rpeer[1:]
    for p in peers:
        pl.semaphore_signal(barrier, inc=1, device_id=p, device_id_type=MESH)
    pl.semaphore_wait(barrier, len(peers))

    after, two, prior = (x + 1) % NX, (x + 2) % NX, (x + 3) % NX

    def source(w):
        return (grads_h, right_root_h)[w % 2].at[w // 2]

    def brow(xx, cc, lo=0, n=ROWS):
        return pl.ds(pl.multiple_of((xx * 2 + cc) * ROWS + lo, 64), n)

    def bcol(xx):
        return pl.ds(pl.multiple_of(xx * 256, 256), 256)

    def x_copy(w, k):
        if w % 2 == 0:
            lo = (0, 64, 64, 0, 0, 64)[k]
            to = (xp, xp, xm, xm, xp, xm)[k]
            if k < 4:
                src, dst = source(w).at[lo : lo + 64], xb.at[w, brow(x, c, lo, 64)]
            else:
                src = dst = xb.at[w, brow(prior if k == 4 else after, c, lo, 64)]
        else:
            to = (xp, xp, xp, xm, xm, xm)[k]
            col = bcol((x, prior, two, x, after, after)[k])
            if k < 5:
                src, dst = source(w).at[:, col], xb.at[w, brow(x, c), col]
            else:
                src = dst = xb.at[w, brow(after, c), col]
        return rcopy(src, dst, xsend.at[w, k], xrecv.at[w, k], to)

    def core_copy(w, i):
        rows = brow((x, prior, after, two)[i], c)
        src = source(w) if i == 0 else xb.at[w, rows]
        return rcopy(src, xb.at[w, rows], xsend.at[w, 6 + i], xrecv.at[w, 6 + i], sibling)

    def own_copy(w):
        return pltpu.make_async_copy(source(w), xb.at[w, brow(x, c)], insem.at[w])

    def x_own(w):
        for k in ((0, 2, 1, 3), (3, 0, 4, 1, 2))[w % 2]:
            x_copy(w, k).start()
        core_copy(w, 0).start()
        own_copy(w).start()

    def x_forward(w):
        for k, on in (((0, 4), (2, 5)), ((3, 5),))[w % 2]:
            x_copy(w, k).wait_recv()
            x_copy(w, on).start()

    def x_rest(w):
        for i, ks in enumerate((((1,), (3,), (4, 5)), ((0, 1, 2), (4,), (5,)))[w % 2]):
            for k in ks:
                x_copy(w, k).wait_recv()
            core_copy(w, 1 + i).start()

    def x_held(w):
        own_copy(w).wait()
        core_copy(w, 0).wait_recv()

    def x_done(w):
        for i in range(1, 4):
            core_copy(w, i).wait_recv()

    def x_drain(w):
        for k in range(6):
            x_copy(w, k).wait_send()
        for i in range(4):
            core_copy(w, i).wait_send()

    def mix(s):
        for m in range(4):
            cols = slice(m * 256, m * 256 + 256)
            mixed[:, cols] = jnp.dot(left_root[s], xb[2 * s, :, cols], preferred_element_type=F32).astype(BF)

    def precondition(s, j):
        w = 2 * s + 1
        at = PLACE.index(j) * 256
        got = jnp.zeros((ROWS, 256), F32)
        for i in range(4):
            lhs = mixed[:, bcol((x + i) % NX)]
            here = i == 0 or (i, j) in ((3, 1), (3, 2), (3, 3), (1, 1), (1, 2), (2, 2))
            r, k = (i, j) if here else (j, i)
            block = xb[w, bcol((x + r) % NX), bcol((x + k) % NX)]
            got += lax.dot_general(
                lhs, block, (((1,), (0 if here else 1,)), ((), ())), preferred_element_type=F32
            )
        got_b = got.astype(BF)
        stack[s, at : at + 128, :] = got_b[:, :128]
        stack[s, at + 128 : at + 256, :] = got_b[:, 128:]
        sq = got * got
        sq = jnp.sum((sq[:, :128] + sq[:, 128:]).reshape(16, 8, 128), axis=0)
        part[2 * s + 1] = sq if j == 0 else part[2 * s + 1] + sq

    def factors(s, keep):
        for m in range(4):
            cols = slice(m * 256, m * 256 + 256)
            outer = lax.dot_general(
                grads[s], xb[2 * s, cols, :], (((1,), (1,)), ((), ())), preferred_element_type=F32
            )
            old = left[s, :, cols].astype(F32)
            left_new[s, :, cols] = jnp.where(keep, 0.95 * old + 0.05 * outer, old).astype(BF)
        mine = xb[2 * s, :, pl.ds(pl.multiple_of(rack * 128, 128), 128)]
        for m in range(4):
            cols = slice(m * 256, m * 256 + 256)
            inner = lax.dot_general(
                mine, xb[2 * s, :, cols], (((0,), (0,)), ((), ())), preferred_element_type=F32
            )
            old = right[s, :, cols].astype(F32)
            new = 0.95 * old + 0.05 * inner
            right_new[s, :, cols] = jnp.where(keep, new, old).astype(BF)

    def graft(s, keep):
        def tile_rows(i, total):
            rows = pl.ds(pl.multiple_of(i * 16, 16), 16)
            g = grads[s, rows, :].astype(F32)
            old = second[s, rows, :].astype(F32)
            moment = 0.95 * old + 0.05 * g * g
            second_new[s, rows, :] = jnp.where(keep, moment, old).astype(BF)
            adam = g / (jnp.sqrt(moment) + 1e-8)
            return total + adam * adam

        total = lax.fori_loop(0, 8, tile_rows, jnp.zeros((16, WIDTH), F32))
        total = jnp.sum(total.reshape(2, 8, WIDTH), axis=0)
        acc = total[:, :128]
        for k in range(1, 8):
            acc = acc + total[:, k * 128 : k * 128 + 128]
        part[2 * s] = acc

    def quarter(k):
        return pl.ds(pl.multiple_of(FIRST_B + QUARTER * k, 16), QUARTER)

    def line_part(s, k, i, sender, receiver):
        if i < 2:
            rows = pl.ds(0, 256) if i == 0 else pl.ds(256, FIRST_B - 256)
        else:
            rows = quarter((receiver + i - 2) % NY)
        return rcopy(
            stack.at[s, rows], ol.at[s * NY + sender, rows], osend.at[s, k - 1, i], orecv.at[s, k - 1, i], ypeer[k]
        )

    def line_copy(s, k, i):
        return line_part(s, k, i, y, (y + k) % NY)

    def line_recv(s, k, i):
        return line_part(s, k, i, (y + NY - k) % NY, y)

    def line_peers(i):
        return (1, 3, 2) if i < 3 else (1, 3)

    def line_send(s, parts):
        for i in parts:
            for k in line_peers(i):
                line_copy(s, k, i).start()

    def onward(s, way, i, to):
        e = s * NY + (to + 2) % NY
        lo = FIRST_B + QUARTER * ((to + i) % NY) + way * HALF_B
        rows = pl.ds(pl.multiple_of(lo, 16), HALF_B)
        return rcopy(ol.at[e, rows], ol.at[e, rows], fsend.at[s, way, i - 1], frecv.at[s, way, i - 1], yn[way])

    def onward_send(s, way, i):
        return onward(s, way, i, (y + (1, 3)[way]) % NY)

    def line_onward(s):
        for i in (3, 4, 5):
            for k in (1, 3):
                line_recv(s, k, i).wait_recv()
        for i in (1, 2, 3):
            for way in range(2):
                onward_send(s, way, i).start()

    def line_pool(s):
        ol[pl.ds(s * NY + y, 1)] = stack[s][None]
        for i in (0, 1, 2):
            for k in (1, 3, 2):
                line_recv(s, k, i).wait_recv()
        for k in range(NY):
            e = s * NY + k
            for way in range(2):
                pool[way, e, :HALF_A] = ol[e, way * HALF_A : way * HALF_A + HALF_A, :]
                lo = pl.multiple_of(FIRST_B + QUARTER * y + way * HALF_B, 16)
                pool[way, e, HALF_A:] = ol[e, pl.ds(lo, HALF_B), :]

    def line_rest(s):
        for i in (1, 2, 3):
            for way in range(2):
                onward(s, way, i, y).wait_recv()
        for k in range(NY):
            e = s * NY + k
            for way in range(2):
                ynear[way, e] = ol[e, quarter((y + (3, 1)[way]) % NY), :]
                lo = pl.multiple_of(FIRST_B + QUARTER * ((y + 2) % NY) + way * HALF_B, 16)
                yopp[way, e] = ol[e, pl.ds(lo, HALF_B), :]

    def z_copy(way, t):
        return rcopy(
            zst.at[way, t % KEEP], zland.at[way, t], zsend.at[way, t % KEEP], zrecv.at[way, t % KEEP], zn[way]
        )

    def n_copy(way, t):
        return rcopy(yst.at[t], ynear.at[way, OWN + t], nsend.at[way, t % KEEP], nrecv.at[way, t % KEEP_Y], yn[way])

    def p_copy(way, t, direct=False):
        half = pl.ds(way * HALF_B, HALF_B)
        src = yst.at[t, half] if direct else ynear.at[way, OWN + t, half]
        to = ypeer[2] if direct else yn[way]
        recv = precv.at[way, KEEP_Y + t - DIRECT if direct else t % KEEP_Y]
        return rcopy(src, yopp.at[way, OWN + t], psend.at[way, t % KEEP], recv, to)

    def o_take(t):
        for way in range(2):
            p_copy(way, t).wait_recv()

    def entry(*at):
        return jnp.clip(table_s[at], 0, OWN + STEPS - 1)

    def z_send(t, again):
        for way in range(2):
            if again:
                z_copy(way, t - KEEP).wait_send()
            zst[way, t % KEEP] = pool[way, entry(way, z, t)]
            z_copy(way, t).start()

    def z_take(t):
        for way in range(2):
            z_copy(way, t).wait_recv()
            pool[way, OWN + t] = zland[way, t]

    def y_send(t, again):
        for way in range(2):
            yst[t, way * HALF_B : way * HALF_B + HALF_B, :] = zland[way, t, HALF_A:, :]
        for way in range(2):
            if again:
                n_copy(way, t - KEEP).wait_send()
            n_copy(way, t).start()

    def y_take(t, again, direct):
        for way in range(2):
            if not direct:
                n_copy(way, t).wait_recv()
            if again:
                p_copy(way, t - KEEP, direct).wait_send()
            p_copy(way, t, direct).start()

    marks = {0, LAG, LAG + LAG_Y, KEEP, KEEP + LAG, KEEP + LAG + LAG_Y, STEPS, STEPS + LAG, DIRECT + LAG, DIRECT + LAG + LAG_Y, LAG + LAG_Y + LAG_O}

    def steps(a, b):
        cuts = [a] + sorted(k for k in marks if a < k < b) + [b]
        for lo, hi in zip(cuts[:-1], cuts[1:]):
            def body(t, _, lo=lo):
                if LAG <= lo < STEPS + LAG:
                    z_take(t - LAG)
                if lo < STEPS:
                    z_send(t, lo >= KEEP)
                if LAG <= lo < STEPS + LAG:
                    y_send(t - LAG, lo - LAG >= KEEP)
                if LAG + LAG_Y <= lo < DIRECT + LAG + LAG_Y:
                    y_take(t - LAG - LAG_Y, lo - LAG - LAG_Y >= KEEP, False)
                if DIRECT + LAG <= lo < STEPS + LAG:
                    y_take(t - LAG, True, True)
                if LAG + LAG_Y + LAG_O <= lo < STEPS + LAG:
                    o_take(t - LAG - LAG_Y - LAG_O)
                return 0

            lax.fori_loop(lo, hi, body, 0)

    def r_copy(k):
        return rcopy(tile.at[0], rk.at[k], rsend.at[k - 1], rrecv.at[k - 1], rpeer[k])

    def sy_copy(k):
        return rcopy(tile.at[1], ry.at[y], sysend.at[k - 1], syrecv.at[k - 1], ypeer[k])

    def sz_copy(k):
        return rcopy(ry, rz.at[z], szsend.at[k - 1], szrecv.at[k - 1], zpeer[k])

    sub = lax.broadcasted_iota(I32, (8, 128), 0)

    def scale_first():
        own = jnp.zeros((8, 128), F32)
        for i in range(4):
            whole = jnp.sum(jnp.sum(part[i], axis=0, keepdims=True), axis=1, keepdims=True)
            own = jnp.where(sub == i, jnp.broadcast_to(whole, (8, 128)), own)
        tile[0] = own
        rk[0] = own
        for k in range(1, 8):
            r_copy(k).start()

    def scale_second():
        for k in range(1, 8):
            r_copy(k).wait_recv()
        total = rk[0]
        for k in range(1, 8):
            total = total + rk[k]
        out = jnp.zeros((8, 128), F32)
        for s in range(2):
            value = jnp.sqrt(total[2 * s : 2 * s + 1]) / jnp.sqrt(total[2 * s + 1 : 2 * s + 2] + 1e-6)
            out = jnp.where(sub == s, jnp.broadcast_to(value, (8, 128)), out)
        tile[1] = out
        ry[pl.ds(y, 1)] = out[None]
        for k in range(1, 4):
            sy_copy(k).start()

    def sy_recv(k):
        frm = (y + NY - k) % NY
        return rcopy(tile.at[1], ry.at[frm], sysend.at[k - 1], syrecv.at[k - 1], ypeer[k])

    def sz_recv(k):
        frm = (z + NZ - k) % NZ
        return rcopy(ry, rz.at[frm], szsend.at[k - 1], szrecv.at[k - 1], zpeer[k])

    def scale_third():
        for k in range(1, 4):
            sy_recv(k).wait_recv()
        rz[pl.ds(z, 1)] = ry[...][None]
        for k in range(1, 8):
            sz_copy(k).start()

    def put(i, src, dst):
        copy = pltpu.make_async_copy(src, dst, outsem.at[i])
        copy.start()
        puts.append(copy)

    puts = []
    x_own(0)
    loads = [
        pltpu.make_async_copy(src, dst, insem.at[4 + i])
        for i, (src, dst) in enumerate(
            [(grads_h, grads), (left_root_h, left_root), (second_h, second), (left_h, left), (right_h, right)]
        )
    ]
    for k in loads:
        k.start()
    to_smem = pltpu.make_async_copy(tables_h, table_s, lsem.at[0])
    to_smem.start()
    x_forward(0)
    x_own(1)
    for k in loads:
        k.wait()
    to_smem.wait()
    held = jnp.zeros((1, 1), I32) + table_s[2, 4, 0]
    graft(0, held > 0)
    graft(1, held > 1)
    put(0, second_new, second_o)
    x_rest(0)
    x_forward(1)
    x_own(2)
    x_held(0)
    x_done(0)
    mix(0)
    x_held(1)
    precondition(0, 0)
    line_send(0, (0,))
    x_rest(1)
    x_done(1)
    for j in (3, 1, 2):
        precondition(0, j)
    line_send(0, (1, 2))
    x_forward(2)
    x_own(3)
    factors(0, held > 0)
    line_pool(0)
    steps(0, 1)
    x_rest(2)
    x_forward(3)
    steps(1, 2)
    x_held(2)
    x_done(2)
    mix(1)
    x_held(3)
    precondition(1, 0)
    line_send(1, (0,))
    steps(2, 4)
    x_rest(3)
    steps(4, 6)
    x_done(3)
    for j in (3, 1, 2):
        precondition(1, j)
    line_send(1, (1, 2))
    scale_first()
    steps(6, SECOND)
    line_pool(1)
    steps(SECOND, SECOND + 3)
    scale_second()
    factors(1, held > 1)
    put(2, left_new, left_o)
    put(3, right_new, right_o)
    steps(SECOND + 3, SECOND + 4)
    line_send(0, (3,))
    steps(SECOND + 4, SECOND + 6)
    line_send(0, (4,))
    scale_third()
    steps(SECOND + 6, SECOND + 8)
    line_send(0, (5,))
    steps(SECOND + 8, SECOND + 10)
    line_send(1, (3,))
    steps(SECOND + 10, SECOND + 12)
    line_send(1, (4,))
    steps(SECOND + 12, SECOND + 14)
    line_onward(0)
    line_send(1, (5,))
    steps(SECOND + 14, SECOND + 20)
    line_onward(1)
    steps(SECOND + 20, SECOND + 26)
    for s in range(2):
        line_rest(s)
    for k in range(1, 8):
        sz_recv(k).wait_recv()
    put(1, rz, sout)
    steps(SECOND + 26, STEPS + LAG)
    for t in range(DIRECT, STEPS):
        for way in range(2):
            n_copy(way, t).wait_recv()
    for t in range(STEPS - LAG_Y - LAG_O, STEPS):
        for way in range(2):
            p_copy(way, t, t >= DIRECT).wait_recv()

    def back(b):
        return pltpu.make_async_copy(rows_out.at[b % 16], blocks_o.at[b], blocksem.at[b % 16])

    def assemble(b, again):
        plus, minus = entry(2, 0, b), entry(2, 1, b)
        if again:
            back(b - 16).wait()
        keep = b % 16
        rows_out[keep, :HALF_A] = pool[0, plus, :HALF_A]
        rows_out[keep, HALF_A:FIRST_B] = pool[1, minus, :HALF_A]

        def fill(q, first, last):
            lo = pl.multiple_of(FIRST_B + QUARTER * (q % NY), 16)
            rows_out[keep, pl.ds(lo, HALF_B)] = first
            rows_out[keep, pl.ds(pl.multiple_of(lo + HALF_B, 16), HALF_B)] = last

        fill(y, pool[0, plus, HALF_A:], pool[1, minus, HALF_A:])
        fill(y + 3, ynear[0, plus, :HALF_B], ynear[0, minus, HALF_B:])
        fill(y + 1, ynear[1, plus, :HALF_B], ynear[1, minus, HALF_B:])
        fill(y + 2, yopp[0, plus], yopp[1, minus])
        back(b).start()
        return 0

    lax.fori_loop(0, 16, lambda b, _: assemble(b, False), 0)
    lax.fori_loop(16, 32, lambda b, _: assemble(b, True), 0)
    for w in range(4):
        x_drain(w)
    for s in range(2):
        for i in range(6):
            for k in line_peers(i):
                line_copy(s, k, i).wait_send()
        for i in (1, 2, 3):
            for way in range(2):
                onward_send(s, way, i).wait_send()
    for t in range(STEPS - KEEP, STEPS):
        for way in range(2):
            z_copy(way, t).wait_send()
            n_copy(way, t).wait_send()
            p_copy(way, t).wait_send()
    for k in range(1, 8):
        r_copy(k).wait_send()
        sz_copy(k).wait_send()
    for k in range(1, 4):
        sy_copy(k).wait_send()
    for p in puts:
        p.wait()
    for b in range(16, 32):
        back(b).wait()


def scale_kernel(
    finds, blocks, scales, left, right, second, out, left_new, right_new, second_new,
    flat, sv, rows_out, held, insem, blocksem, outsem,
):
    _, _, x, _ = me()
    first = pltpu.make_async_copy(scales, sv, insem.at[3])
    first.start()

    def fetch(b):
        return pltpu.make_async_copy(blocks.at[b], flat.at[b], blocksem.at[b])

    def begin(b, _):
        fetch(b).start()
        return 0

    lax.fori_loop(0, 8, begin, 0)
    through = [
        pltpu.make_async_copy(ref, held.at[i], insem.at[i]) for i, ref in enumerate((left, right, second))
    ]
    for k in through:
        k.start()
    lax.fori_loop(8, 32, begin, 0)
    first.wait()

    def back(b):
        return pltpu.make_async_copy(rows_out.at[b % 8], out.at[b], outsem.at[b % 8])

    def one(b, again):
        owner = jnp.clip(finds[2, b], 0, NY * NZ - 1)
        scale = sv[owner // NY, owner % NY, pl.ds(jnp.clip(finds[3, b], 0, 1), 1), :]
        fetch(b).wait()
        if again:
            back(b - 8).wait()
        for i, j in enumerate(PLACE):
            for half in range(2):
                row = (2 * i + half) * 128
                col = pl.multiple_of((x + j) % NX * 256 + half * 128, 128)
                part = flat[b, row : row + 128, :].astype(F32) * scale
                rows_out[b % 8, :, pl.ds(col, 128)] = part.astype(BF)
        back(b).start()
        return 0

    lax.fori_loop(0, 8, lambda b, _: one(b, False), 0)
    for i, ref in enumerate((left_new, right_new, second_new)):
        through[i].wait()
        through[i] = pltpu.make_async_copy(held.at[i], ref, insem.at[i])
        through[i].start()
    lax.fori_loop(8, 32, lambda b, _: one(b, True), 0)
    for b in range(24, 32):
        back(b).wait()
    for k in through:
        k.wait()


def on_device(grads, left, right, left_root, right_root, second, owner):
    smem, hbm = pl.BlockSpec(memory_space=pltpu.SMEM), pl.BlockSpec(memory_space=pl.ANY)
    vmem = pl.BlockSpec(memory_space=pltpu.VMEM)
    shape = jax.ShapeDtypeStruct
    b_shape = (SLOTS_DEV, ROWS, WIDTH)
    block = shape(b_shape, BF)
    tables, finds, which = pl.pallas_call(
        plan_kernel,
        out_shape=(shape((3, 8, 128), I32), shape((8, 128), I32), shape((1,), I32)),
        in_specs=[smem],
        out_specs=(vmem, vmem, smem),
        name="plan",
    )(owner)
    s_shape = (NZ, NY, 8, 128)
    dma = pltpu.SemaphoreType.DMA
    stacked = (32, WIDTH, 128)

    def run(i, *args):
        STEPS = VARIANTS[i]
        entries = OWN + STEPS
        return pl.pallas_call(
            functools.partial(main_kernel, STEPS),
            out_shape=(
                block, block, block, shape(stacked, BF), shape(s_shape, F32),
            ),
            in_specs=[hbm] * 7,
            out_specs=(hbm,) * 5,
            scratch_shapes=[pltpu.VMEM(b_shape, BF)] * 8
            + [
                pltpu.VMEM((4, WIDTH, WIDTH), BF),
                pltpu.VMEM((ROWS, WIDTH), BF),
                pltpu.VMEM((SLOTS_DEV, WIDTH, 128), BF),
                pltpu.VMEM((OWN, WIDTH, 128), BF),
                pltpu.VMEM((2, STEPS, CHUNK, 128), BF),
                pltpu.VMEM((2, entries, CHUNK, 128), BF),
                pltpu.VMEM((2, KEEP, CHUNK, 128), BF),
                pltpu.VMEM((STEPS, QUARTER, 128), BF),
                pltpu.VMEM((2, entries, QUARTER, 128), BF),
                pltpu.VMEM((2, entries, HALF_B, 128), BF),
                pltpu.VMEM((16, WIDTH, 128), BF),
                pltpu.SMEM((3, 8, 128), I32),
                pltpu.VMEM((4, 8, 128), F32),
                pltpu.VMEM((8, 8, 128), F32),
                pltpu.VMEM((NY, 8, 128), F32),
                pltpu.VMEM(s_shape, F32),
                pltpu.VMEM((2, 8, 128), F32),
                dma((4, 10)), dma((4, 10)),
                dma((2, 3, 6)), dma((2, 3, 6)), dma((2, 2, 3)), dma((2, 2, 3)),
                dma((2, KEEP)), dma((2, KEEP)),
                dma((2, KEEP)), dma((2, KEEP_Y)),
                dma((2, KEEP)), dma((2, KEEP_Y + LAST)),
                dma((7,)), dma((7,)), dma((3,)), dma((3,)), dma((7,)), dma((7,)),
                dma((1,)), dma((9,)), dma((4,)), dma((16,)),
            ],
            compiler_params=pltpu.CompilerParams(
                collective_id=1 + i, has_side_effects=True, vmem_limit_bytes=60 << 20
            ),
            name="shampoo",
        )(*args)

    left_new, right_new, second_new, blocks, scales = lax.switch(
        which[0],
        [functools.partial(run, i) for i in range(len(VARIANTS))],
        grads, left, right, left_root, right_root, second, tables,
    )
    directions, left_new, right_new, second_new = pl.pallas_call(
        scale_kernel,
        out_shape=(shape((32, ROWS, WIDTH), BF), block, block, block),
        in_specs=[smem] + [hbm] * 5,
        out_specs=(hbm,) * 4,
        scratch_shapes=[
            pltpu.VMEM(stacked, BF),
            pltpu.VMEM(s_shape, F32),
            pltpu.VMEM((8, ROWS, WIDTH), BF),
            pltpu.VMEM((3, *b_shape), BF),
            dma((4,)), dma((32,)), dma((8,)),
        ],
        compiler_params=pltpu.CompilerParams(vmem_limit_bytes=60 << 20),
        name="spread",
    )(finds, blocks, scales, left_new, right_new, second_new)
    return (left_new, right_new, second_new, directions)


def solution(mesh):
    block = P("rep", "rack", None)
    return jax.shard_map(
        on_device,
        mesh=mesh,
        in_specs=(block,) * 6 + (P(),),
        out_specs=(block, block, block, P(None, "rack", None)),
        check_vma=False,
    )
```
